32 devices in a mesh: seq: 8 (over z, y), head: 4 (over x, core).
Axes of the slice: x: 2, y: 2, z: 4, core: 2. Of those that a mesh axis runs over, the one named last changes fastest.
Arguments:
- queries: bfloat16 [2, 512, 2048], P(None, 'seq', 'head'), may hold values from -6 to 6
- keys: bfloat16 [2, 512, 2048], P(None, 'seq', 'head'), may hold values from -6 to 6
- values: bfloat16 [2, 512, 2048], P(None, 'seq', 'head'), may hold values from -6 to 6
- out_weight: bfloat16 [2048, 4096], P('head'), may hold values from -0.125 to 0.125
- upstream: bfloat16 [2, 512, 4096], P(None, 'seq', 'head'), may hold values from -6 to 6
Outputs:
- output: bfloat16 [2, 512, 4096], P(None, 'seq', 'head')
- query_grad: bfloat16 [2, 512, 2048], P(None, 'seq', 'head')
- key_grad: bfloat16 [2, 512, 2048], P(None, 'seq', 'head')
- value_grad: bfloat16 [2, 512, 2048], P(None, 'seq', 'head')
- weight_grad: float32 [2048, 4096], P('head', 'seq')
The draws below stay inside these ranges and needn't reach their ends.
All inputs are finite; a program needn't handle non-finite values.
Results may differ from the reference program's by a relative error of at most 0.01405.
Values may be sent and summed in bfloat16 or wider, within the bound.
No kernel may reach another device: no remote copies, remote signals or barrier semaphores. Data moves between devices by JAX's collectives and lax.ppermute only.
A program may use at most 128 MiB of HBM per device.

```python
import jax
import jax.numpy as jnp
from jax import lax

D = 4096
HEADS = 16
HEAD_DIM = 128
SPAN = 64
HD = 2048
HALF = 512
N_SEQ = 8


def raised(entries, key, source, target, shards_of, factor):
    def block_of(dim):
        return (jnp.arange(entries.shape[dim]) // (entries.shape[dim] // shards_of)).reshape((-1,) + (1,) * (entries.ndim - 1 - dim))

    near = jax.random.permutation(key, shards_of)[block_of(target)]
    second = (block_of(target) + shards_of // 2) % shards_of
    return jnp.where((block_of(source) == near) | (block_of(source) == second), factor * entries, entries)


def block_scale(stream_key, dims, cuts, low, largest):
    factor_of, own = 1.0, jax.random.fold_in(stream_key, 6)
    for dim, blocks in cuts:
        steps = jnp.exp(jax.random.uniform(jax.random.fold_in(own, dim), (blocks,), jnp.float32, low / len(cuts), largest / len(cuts)))
        factor_of = factor_of * jnp.repeat(steps, dims[dim] // blocks).reshape([-1 if axis == dim else 1 for axis in range(len(dims))])
    return factor_of


def centred(own_key, shape, scale, bound, shards=(), kind=jnp.bfloat16):
    entries = jax.random.normal(own_key, shape, jnp.float32) * scale
    if len(shards) > 0:
        entries = block_scale(own_key, shape, shards, -0.22, 0.18) * entries
    return jnp.clip(entries, min=-bound, max=bound).astype(kind)


def heavy_noise(stream_key, dims, scale, reach, cuts, heavy, dtype=jnp.bfloat16):
    drawn = scale * jax.random.normal(stream_key, dims, jnp.float32)
    if cuts:
        drawn = drawn * block_scale(stream_key, dims, cuts, -0.22, 0.18)
    return jnp.clip(raised(drawn, jax.random.fold_in(stream_key, 3), *heavy), -reach, reach).astype(dtype)


def setup_inputs(seed: int = 0) -> dict:
    splits = jax.random.split(jax.random.key(seed), 6)
    return {
        "queries": centred(splits[0], (2, HALF, HD), 1.0, 6.0, ((1, 8), (2, 4))),
        "keys": centred(splits[1], (2, HALF, HD), 1.0, 6.0, ((1, 8), (2, 4))),
        "values": centred(splits[2], (2, HALF, HD), 1.0, 6.0, ((1, 8), (2, 4))),
        "out_weight": centred(splits[3], (HD, D), HD ** -0.5, 0.125, ((0, 4),)),
        "upstream": heavy_noise(splits[4], (2, HALF, D), 1.0, 6.0, ((1, 8), (2, 4)), (1, 2, 8, 2.0)),
    }


eps = 1e-06

def natural(arr):
    width = arr.shape[-1]
    blocks = arr[1].reshape(N_SEQ, SPAN, width)[::-1].reshape(N_SEQ * SPAN, width)
    return jnp.concatenate([arr[0], blocks], axis=0)

def to_pairs(arr):
    half = arr.shape[0] // 2
    width = arr.shape[-1]
    second = arr[half:].reshape(N_SEQ, SPAN, width)[::-1].reshape(half, width)
    return jnp.stack([arr[:half], second])

def lower_mask():
    rows = lax.broadcasted_iota(jnp.int32, (SPAN, SPAN), 0)
    cols = lax.broadcasted_iota(jnp.int32, (SPAN, SPAN), 1)
    return rows >= cols

def head_states(query, key, value):
    qf = query.astype(jnp.float32)
    kf = key.astype(jnp.float32)
    vf = value.astype(jnp.float32)
    kv_terms = jnp.einsum('ncd,nce->nde', kf, vf)
    summed = jnp.cumsum(kv_terms, axis=0)[:-1]
    states = jnp.concatenate([jnp.zeros_like(kv_terms[:1]), summed], axis=0).astype(jnp.bfloat16)
    weights = jnp.where(lower_mask(), jnp.einsum('ntd,nsd->nts', qf, kf), 0.0).astype(jnp.bfloat16)
    return (qf, kf, vf, states, weights)

def forward_head(operands):
    query, key, value = operands
    qf, kf, vf, states, weights = head_states(query, key, value)
    return jnp.einsum('nts,nse->nte', weights.astype(jnp.float32), vf) + jnp.einsum('ntd,nde->nte', qf, states.astype(jnp.float32))

def backward_head(operands):
    query, key, value, grad = operands
    qf, kf, vf, states, weights = head_states(query, key, value)
    gf = grad.astype(jnp.float32)
    qg_terms = jnp.einsum('ncd,nce->nde', qf, gf)
    reverse_sum = jnp.cumsum(qg_terms[::-1], axis=0)[::-1]
    later = jnp.concatenate([reverse_sum[1:], jnp.zeros_like(qg_terms[:1])], axis=0).astype(jnp.bfloat16)
    laterf = later.astype(jnp.float32)
    diffs = jnp.where(lower_mask(), jnp.einsum('nte,nse->nts', gf, vf), 0.0).astype(jnp.bfloat16)
    diffsf = diffs.astype(jnp.float32)
    query_grad = jnp.einsum('nts,nsd->ntd', diffsf, kf) + jnp.einsum('nte,nde->ntd', gf, states.astype(jnp.float32))
    key_grad = jnp.einsum('nts,ntd->nsd', diffsf, qf) + jnp.einsum('nse,nde->nsd', vf, laterf)
    value_grad = jnp.einsum('nts,nte->nse', weights.astype(jnp.float32), gf) + jnp.einsum('nsd,nde->nse', kf, laterf)
    return (query_grad.astype(jnp.bfloat16), key_grad.astype(jnp.bfloat16), value_grad.astype(jnp.bfloat16))

def reference(queries, keys, values, out_weight, upstream):
    blocks = 2 * N_SEQ

    def by_head(arr):
        return natural(arr).reshape(blocks, SPAN, HEADS, HEAD_DIM).transpose(2, 0, 1, 3)

    def by_rows(arr):
        return to_pairs(arr.transpose(1, 2, 0, 3).reshape(blocks * SPAN, HEADS * HEAD_DIM))
    query_heads = by_head(queries)
    key_heads = by_head(keys)
    value_heads = by_head(values)
    attended = lax.map(forward_head, (query_heads, key_heads, value_heads))
    scale = jnp.sqrt(lax.optimization_barrier(jnp.mean(attended * attended, axis=-1, keepdims=True)) + eps)
    normed = attended / scale
    hidden = normed.astype(jnp.bfloat16).transpose(1, 2, 0, 3).reshape(blocks * SPAN, HEADS * HEAD_DIM)
    output = jnp.dot(hidden, out_weight, preferred_element_type=jnp.float32).astype(jnp.bfloat16)
    full_up = natural(upstream)
    hidden_grad = jnp.dot(full_up, out_weight.T, preferred_element_type=jnp.float32)
    weight_grad = jnp.dot(hidden.T, full_up, preferred_element_type=jnp.float32)
    grad_heads = hidden_grad.reshape(blocks, SPAN, HEADS, HEAD_DIM).transpose(2, 0, 1, 3)
    inner = lax.optimization_barrier(jnp.mean(grad_heads * normed, axis=-1, keepdims=True))
    attn_grad = ((grad_heads - normed * inner) / scale).astype(jnp.bfloat16)
    query_grad, key_grad, value_grad = lax.map(backward_head, (query_heads, key_heads, value_heads, attn_grad))
    return (to_pairs(output), by_rows(query_grad), by_rows(key_grad), by_rows(value_grad), weight_grad)
```

```python
import functools

import jax
import jax.numpy as jnp
from jax import lax
from jax.experimental import pallas as pl
from jax.experimental.pallas import tpu as pltpu
from jax.sharding import PartitionSpec as P

HEAD_DIM = 128
EPS = 1e-06

NN = (((1,), (0,)), ((), ()))
NT = (((1,), (1,)), ((), ()))
TN = (((0,), (0,)), ((), ()))


def mm(a, b, dims):
    return lax.dot_general(a, b, dims, preferred_element_type=jnp.float32)


def head_cols(i):
    return slice(i * HEAD_DIM, (i + 1) * HEAD_DIM)


def lower(length):
    rows = lax.broadcasted_iota(jnp.int32, (length, length), 0)
    cols = lax.broadcasted_iota(jnp.int32, (length, length), 1)
    return rows >= cols


def xor_permute(x, axis, bit):
    count = lax.axis_size(axis)
    return lax.ppermute(x, axis, [(i, i ^ bit) for i in range(count)])


def whole(n):
    return [pl.BlockSpec(memory_space=pltpu.VMEM)] * n


def kernel_call(body, outs, args, flops=0, vmem=32 * 2**20):
    moved = sum(a.size * a.dtype.itemsize for a in list(args) + list(outs))
    return pl.pallas_call(
        body,
        out_shape=outs,
        in_specs=whole(len(args)),
        out_specs=whole(len(outs)),
        compiler_params=pltpu.CompilerParams(vmem_limit_bytes=vmem),
        cost_estimate=pl.CostEstimate(flops=flops, bytes_accessed=moved, transcendentals=0),
    )(*args)


def shaped(shape, dtype):
    return jax.ShapeDtypeStruct(shape, dtype)


def kv_body(k_ref, v_ref, own_ref, send_ref):
    for i in range(k_ref.shape[2] // HEAD_DIM):
        c = head_cols(i)
        first = mm(k_ref[0, :, c], v_ref[0, :, c], TN)
        second = mm(k_ref[1, :, c], v_ref[1, :, c], TN)
        own_ref[i] = first
        send_ref[0, i] = first.astype(jnp.bfloat16)
        send_ref[1, i] = (first + second).astype(jnp.bfloat16)


def exchange(near, send, axis):
    count = lax.axis_size(axis)
    place = lax.axis_index(axis)
    below = jnp.zeros_like(near)
    above = jnp.zeros_like(near)
    group = send.astype(jnp.float32)
    bit = 1
    while bit < count:
        upper = (place & bit) != 0
        if 2 * bit < count:
            got = xor_permute(send, axis, bit).astype(jnp.float32)
            got_near, got_both = got[0], got[1]
            group = group + got
            send = group.astype(jnp.bfloat16)
        else:
            got = xor_permute(jnp.where(upper, send[1], send[0]), axis, bit).astype(jnp.float32)
            got_near = got_both = got
        below = jnp.where(upper, below + got_near, below)
        above = jnp.where(upper, above, above + got_both)
        bit *= 2
    return below, above


def grad_body(heads, index_ref, *refs):
    chunks, w_ref, out_ref = refs[:heads], refs[heads], refs[heads + 1]
    step = pl.program_id(0)
    for m in range(heads):

        @pl.when(step == m)
        def _(m=m):
            part = mm(chunks[m][...], w_ref[...], NT)
            if m == 0:
                out_ref[...] = part
            else:
                out_ref[...] += part


def hidden_grad_of(chunks, weight, place):
    n = len(chunks)
    rows, cols = chunks[0].shape
    features = weight.shape[0]
    index = place ^ jnp.arange(n, dtype=jnp.int32)
    return pl.pallas_call(
        functools.partial(grad_body, n),
        out_shape=shaped((rows, features), jnp.float32),
        grid_spec=pltpu.PrefetchScalarGridSpec(
            num_scalar_prefetch=1,
            grid=(n,),
            in_specs=[pl.BlockSpec((rows, cols), lambda m, ix: (0, 0))] * n
            + [pl.BlockSpec((features, cols), lambda m, ix: (0, ix[m]))],
            out_specs=pl.BlockSpec((rows, features), lambda m, ix: (0, 0)),
        ),
        compiler_params=pltpu.CompilerParams(vmem_limit_bytes=32 * 2**20),
        cost_estimate=pl.CostEstimate(
            flops=2 * rows * features * cols * n,
            bytes_accessed=weight.size * 2 + n * rows * cols * 2,
            transcendentals=0,
        ),
    )(index, *chunks, weight)


def forward_body(q_ref, k_ref, v_ref, hg_ref, own_ref, below_ref, above_ref,
                 state_ref, hidden_ref, g_ref, qown_ref, qsend_ref):
    length = q_ref.shape[1]
    mask = lower(length)
    for i in range(q_ref.shape[2] // HEAD_DIM):
        c = head_cols(i)
        below = below_ref[i]
        states = (below, below + own_ref[i] + above_ref[i])
        terms = []
        for p in range(2):
            r = slice(p * length, (p + 1) * length)
            q, k, v = q_ref[p, :, c], k_ref[p, :, c], v_ref[p, :, c]
            state = states[p].astype(jnp.bfloat16)
            state_ref[p, i] = state
            weights = jnp.where(mask, mm(q, k, NT), 0.0).astype(jnp.bfloat16)
            attended = mm(weights, v, NN) + mm(q, state, NN)
            scale = jnp.sqrt(jnp.mean(attended * attended, axis=-1, keepdims=True) + EPS)
            normed = attended / scale
            hidden_ref[r, c] = normed.astype(jnp.bfloat16)
            hg = hg_ref[r, c]
            inner = jnp.mean(hg * normed, axis=-1, keepdims=True)
            g = ((hg - normed * inner) / scale).astype(jnp.bfloat16)
            g_ref[p, :, c] = g
            terms.append(mm(q, g, TN))
        qown_ref[i] = terms[1]
        qsend_ref[0, i] = terms[1].astype(jnp.bfloat16)
        qsend_ref[1, i] = (terms[0] + terms[1]).astype(jnp.bfloat16)


def inside_body(q_ref, k_ref, v_ref, g_ref, state_ref, dq_ref, dk_ref, dv_ref):
    length = q_ref.shape[1]
    mask = lower(length)
    for i in range(q_ref.shape[2] // HEAD_DIM):
        c = head_cols(i)
        for p in range(2):
            q, k, v, g = q_ref[p, :, c], k_ref[p, :, c], v_ref[p, :, c], g_ref[p, :, c]
            weights = jnp.where(mask, mm(q, k, NT), 0.0).astype(jnp.bfloat16)
            diffs = jnp.where(mask, mm(g, v, NT), 0.0).astype(jnp.bfloat16)
            dq_ref[p, :, c] = (mm(diffs, k, NN) + mm(g, state_ref[p, i], NT)).astype(jnp.bfloat16)
            dk_ref[p, :, c] = mm(diffs, q, TN)
            dv_ref[p, :, c] = mm(weights, g, TN)


def final_body(k_ref, v_ref, dkp_ref, dvp_ref, own_ref, below_ref, above_ref, dk_ref, dv_ref):
    for i in range(k_ref.shape[2] // HEAD_DIM):
        c = head_cols(i)
        below = below_ref[i]
        laters = (below + own_ref[i] + above_ref[i], below)
        for p in range(2):
            later = laters[p].astype(jnp.bfloat16)
            k, v = k_ref[p, :, c], v_ref[p, :, c]
            dk_ref[p, :, c] = (dkp_ref[p, :, c] + mm(v, later, NT)).astype(jnp.bfloat16)
            dv_ref[p, :, c] = (dvp_ref[p, :, c] + mm(k, later, NN)).astype(jnp.bfloat16)


def project_body(hidden_ref, w_ref, out_ref):
    out_ref[...] = mm(hidden_ref[...], w_ref[...], NN).astype(jnp.bfloat16)


def project(hidden, weight):
    rows, features = hidden.shape
    cols = weight.shape[1]
    tile = min(1024, cols)
    return pl.pallas_call(
        project_body,
        out_shape=shaped((rows, cols), jnp.bfloat16),
        grid=(cols // tile,),
        in_specs=[
            pl.BlockSpec((rows, features), lambda m: (0, 0)),
            pl.BlockSpec((features, tile), lambda m: (0, m)),
        ],
        out_specs=pl.BlockSpec((rows, tile), lambda m: (0, m)),
        compiler_params=pltpu.CompilerParams(vmem_limit_bytes=32 * 2**20),
        cost_estimate=pl.CostEstimate(
            flops=2 * rows * features * cols,
            bytes_accessed=2 * (hidden.size + weight.size + rows * cols),
            transcendentals=0,
        ),
    )(hidden, weight)


def weight_body(slots, index_ref, *refs):
    hidden_refs, up_ref, out_ref = refs[:-2], refs[-2], refs[-1]
    total = None
    for m in range(slots):
        up = up_ref[index_ref[m]]
        part = mm(hidden_refs[m][...], up, TN)
        total = part if total is None else total + part
    out_ref[...] = total


def weight_grad_of(hiddens, ups, index):
    n = len(hiddens)
    rows, features = hiddens[0].shape
    cols = ups.shape[2]
    return pl.pallas_call(
        functools.partial(weight_body, n),
        out_shape=shaped((features, cols), jnp.float32),
        in_specs=[pl.BlockSpec(memory_space=pltpu.SMEM)] + whole(n + 1),
        out_specs=pl.BlockSpec(memory_space=pltpu.VMEM),
        compiler_params=pltpu.CompilerParams(vmem_limit_bytes=32 * 2**20),
        cost_estimate=pl.CostEstimate(
            flops=2 * n * rows * features * cols,
            bytes_accessed=2 * n * rows * (features + cols) + 4 * features * cols,
            transcendentals=0,
        ),
    )(index, *hiddens, ups)


def gather_xor(x, axis):
    count = lax.axis_size(axis)
    slots = {0: x}
    bit = count // 2
    while bit:
        for m in list(slots):
            slots[m ^ bit] = xor_permute(slots[m], axis, bit)
        bit //= 2
    return [slots[m] for m in range(count)]


def on_device(queries, keys, values, out_weight, upstream):
    pair, length, width = queries.shape
    heads = width // HEAD_DIM
    n_seq, n_head = lax.axis_size("seq"), lax.axis_size("head")
    seq, head = lax.axis_index("seq"), lax.axis_index("head")
    rows = pair * length
    f32, bf16 = jnp.float32, jnp.bfloat16
    square = (heads, HEAD_DIM, HEAD_DIM)
    product = 2 * rows * HEAD_DIM * width

    kv_own, kv_send = kernel_call(
        kv_body, (shaped(square, f32), shaped((2,) + square, bf16)), (keys, values), product
    )
    below, above = exchange(kv_own, kv_send, "seq")

    flat_up = upstream.reshape(rows, upstream.shape[2])
    chunks = gather_xor(flat_up, "head")
    hidden_grad = hidden_grad_of(chunks, out_weight, head)

    states, hidden, attn_grad, qg_own, qg_send = kernel_call(
        forward_body,
        (
            shaped((2,) + square, bf16),
            shaped((rows, width), bf16),
            shaped((pair, length, width), bf16),
            shaped(square, f32),
            shaped((2,) + square, bf16),
        ),
        (queries, keys, values, hidden_grad, kv_own, below, above),
        3 * product,
    )
    q_below, q_above = exchange(qg_own, qg_send, "seq")

    output = lax.psum_scatter(project(hidden, out_weight), "head", scatter_dimension=1, tiled=True)

    query_grad, key_part, value_part = kernel_call(
        inside_body,
        (
            shaped((pair, length, width), bf16),
            shaped((pair, length, width), f32),
            shaped((pair, length, width), f32),
        ),
        (queries, keys, values, attn_grad, states),
        4 * product,
    )
    key_grad, value_grad = kernel_call(
        final_body,
        (shaped((pair, length, width), bf16), shaped((pair, length, width), bf16)),
        (keys, values, key_part, value_part, qg_own, q_below, q_above),
        2 * product,
    )

    if n_seq == 2 * n_head:
        cols = flat_up.shape[1] // 2
        odd = seq & 1
        left, right = flat_up[:, :cols], flat_up[:, cols:]
        flip = odd == 1
        got = []
        for k in range(2):
            pairs = [
                (s * n_head + h, (2 * h + (k ^ (s & 1))) * n_head + s // 2)
                for s in range(n_seq)
                for h in range(n_head)
            ]
            piece = jnp.where(flip, left if k else right, right if k else left)
            got.append(lax.ppermute(piece, ("seq", "head"), pairs))
        ups = lax.all_gather(jnp.stack(got), "head").reshape(n_seq, rows, cols)
        hiddens = gather_xor(hidden, "seq")
        source = seq ^ jnp.arange(n_seq, dtype=jnp.int32)
        index = (source // 2) * 2 + ((source & 1) ^ odd)
        weight_grad = weight_grad_of(hiddens, ups, index)
    else:
        full_up = lax.all_gather(flat_up, "head", axis=1, tiled=True)
        weight_grad = lax.psum_scatter(
            mm(full_up, hidden, TN), "seq", scatter_dimension=0, tiled=True
        ).T

    return (
        output.reshape(pair, length, -1),
        query_grad,
        key_grad,
        value_grad,
        weight_grad,
    )


def solution(mesh):
    rows = P(None, "seq", "head")
    return jax.shard_map(
        on_device,
        mesh=mesh,
        in_specs=(rows, rows, rows, P("head", None), rows),
        out_specs=(rows, rows, rows, rows, P("head", "seq")),
        check_vma=False,
    )
```

```python
import functools

import jax
import jax.numpy as jnp
from jax import lax
from jax.experimental import pallas as pl
from jax.experimental.pallas import tpu as pltpu
from jax.sharding import PartitionSpec as P

HEAD_DIM = 128
EPS = 1e-06

NN = (((1,), (0,)), ((), ()))
NT = (((1,), (1,)), ((), ()))
TN = (((0,), (0,)), ((), ()))


def mm(a, b, dims):
    return lax.dot_general(a, b, dims, preferred_element_type=jnp.float32)


def head_cols(i):
    return slice(i * HEAD_DIM, (i + 1) * HEAD_DIM)


def lower(length):
    rows = lax.broadcasted_iota(jnp.int32, (length, length), 0)
    cols = lax.broadcasted_iota(jnp.int32, (length, length), 1)
    return rows >= cols


def xor_permute(x, axis, bit):
    count = lax.axis_size(axis)
    return lax.ppermute(x, axis, [(i, i ^ bit) for i in range(count)])


def whole(n):
    return [pl.BlockSpec(memory_space=pltpu.VMEM)] * n


def lasting(us):
    return pl.CostEstimate(flops=int(us * 1.1e9), bytes_accessed=0, transcendentals=0)


def kernel_call(body, outs, args, us=0.5, vmem=16 * 2**20):
    return pl.pallas_call(
        body,
        out_shape=outs,
        in_specs=whole(len(args)),
        out_specs=whole(len(outs)),
        compiler_params=pltpu.CompilerParams(vmem_limit_bytes=vmem),
        cost_estimate=lasting(us),
    )(*args)


def shaped(shape, dtype):
    return jax.ShapeDtypeStruct(shape, dtype)


def kv_body(k_hbm, v_hbm, own_ref, send_ref, k_ref, v_ref, sems):
    loads = [
        pltpu.make_async_copy(k_hbm, k_ref, sems.at[0]),
        pltpu.make_async_copy(v_hbm, v_ref, sems.at[1]),
    ]
    for load in loads:
        load.start()
    for load in loads:
        load.wait()
    for i in range(k_ref.shape[2] // HEAD_DIM):
        c = head_cols(i)
        first = mm(k_ref[0, :, c], v_ref[0, :, c], TN)
        second = mm(k_ref[1, :, c], v_ref[1, :, c], TN)
        own_ref[i] = first
        send_ref[0, i] = first.astype(jnp.bfloat16)
        send_ref[1, i] = (first + second).astype(jnp.bfloat16)


def in_hbm(x):
    return pltpu.with_memory_space_constraint(x, pltpu.HBM)


def kv_products(keys, values):
    heads = keys.shape[2] // HEAD_DIM
    square = (heads, HEAD_DIM, HEAD_DIM)
    return pl.pallas_call(
        kv_body,
        out_shape=(shaped(square, jnp.float32), shaped((2,) + square, jnp.bfloat16)),
        in_specs=[pl.BlockSpec(memory_space=pltpu.HBM)] * 2,
        out_specs=whole(2),
        scratch_shapes=[
            pltpu.VMEM(keys.shape, keys.dtype),
            pltpu.VMEM(values.shape, values.dtype),
            pltpu.SemaphoreType.DMA((2,)),
        ],
        compiler_params=pltpu.CompilerParams(vmem_limit_bytes=16 * 2**20),
    )(keys, values)


class Rounds:
    def __init__(self, near, send, axis, ahead):
        count = lax.axis_size(axis)
        place = lax.axis_index(axis)
        below = jnp.zeros_like(near)
        above = jnp.zeros_like(near)
        group = send.astype(jnp.float32)
        self.sent = []
        bit = 1
        while bit < count:
            upper = (place & bit) != 0
            last = 2 * bit == count
            if last:
                send = jnp.where(upper, send[1], send[0])
            if bit in ahead:
                send = after(send, *ahead[bit])
            self.sent.append(send)
            got = xor_permute(send, axis, bit).astype(jnp.float32)
            got_near, got_both = (got, got) if last else (got[0], got[1])
            below = jnp.where(upper, below + got_near, below)
            above = jnp.where(upper, above, above + got_both)
            if not last:
                group = group + got
                send = group.astype(jnp.bfloat16)
            bit *= 2
        self.below, self.above = below, above


def pick(table, at):
    value = jnp.int32(table[0])
    for i, entry in enumerate(table[1:], 1):
        value = jnp.where(at == i, entry, value)
    return value


def near_body(spot_ref, w_hbm, up_hbm, out_ref, w_ref, up_ref, sems):
    n, _, cols = w_ref.shape
    loads = [pltpu.make_async_copy(up_hbm, up_ref, sems.at[n])]
    for slot in range(n):
        at = pl.multiple_of((spot_ref[1] ^ slot) * cols, cols)
        loads.append(pltpu.make_async_copy(w_hbm.at[:, pl.ds(at, cols)], w_ref.at[slot], sems.at[slot]))
    for load in loads:
        load.start()
    loads[0].wait()
    loads[1].wait()
    out_ref[...] = mm(up_ref[...], w_ref[0], NT)
    for load in loads[2:]:
        load.wait()


def near_grad_of(up, weight, spot, n):
    rows, cols = up.shape
    features = weight.shape[0]
    return pl.pallas_call(
        near_body,
        out_shape=(
            shaped((rows, features), jnp.float32),
            shaped((n, features, cols), weight.dtype),
            shaped(up.shape, up.dtype),
        ),
        in_specs=[pl.BlockSpec(memory_space=pltpu.SMEM)] + [pl.BlockSpec(memory_space=pltpu.HBM)] * 2,
        out_specs=whole(3),
        scratch_shapes=[pltpu.SemaphoreType.DMA((n + 1,))],
        compiler_params=pltpu.CompilerParams(vmem_limit_bytes=16 * 2**20),
        cost_estimate=lasting(3),
    )(spot, weight, up)


def far_body(slots, w_ref, before_ref, *refs):
    chunks, out_ref = refs[:-1], refs[-1]
    total = before_ref[...]
    for i, slot in enumerate(slots):
        total += mm(chunks[i][...], w_ref[slot], NT)
    out_ref[...] = total


def forward_body(q_ref, k_ref, v_ref, hg_ref, own_ref, below_ref, above_ref,
                 state_ref, hidden_ref, g_ref, qown_ref, qsend_ref):
    length = q_ref.shape[1]
    mask = lower(length)
    for i in range(q_ref.shape[2] // HEAD_DIM):
        c = head_cols(i)
        below = below_ref[i]
        states = (below, below + own_ref[i] + above_ref[i])
        terms = []
        for p in range(2):
            r = slice(p * length, (p + 1) * length)
            q, k, v = q_ref[p, :, c], k_ref[p, :, c], v_ref[p, :, c]
            state = states[p].astype(jnp.bfloat16)
            state_ref[p, i] = state
            weights = jnp.where(mask, mm(q, k, NT), 0.0).astype(jnp.bfloat16)
            attended = mm(weights, v, NN) + mm(q, state, NN)
            scale = jnp.sqrt(jnp.mean(attended * attended, axis=-1, keepdims=True) + EPS)
            normed = attended / scale
            hidden_ref[r, c] = normed.astype(jnp.bfloat16)
            hg = hg_ref[r, c]
            inner = jnp.mean(hg * normed, axis=-1, keepdims=True)
            g = ((hg - normed * inner) / scale).astype(jnp.bfloat16)
            g_ref[p, :, c] = g
            terms.append(mm(q, g, TN))
        qown_ref[i] = terms[1]
        qsend_ref[0, i] = terms[1].astype(jnp.bfloat16)
        qsend_ref[1, i] = (terms[0] + terms[1]).astype(jnp.bfloat16)


def inside_body(q_ref, k_ref, v_ref, g_ref, state_ref, dq_ref, dk_ref, dv_ref):
    length = q_ref.shape[1]
    mask = lower(length)
    for i in range(q_ref.shape[2] // HEAD_DIM):
        c = head_cols(i)
        for p in range(2):
            q, k, v, g = q_ref[p, :, c], k_ref[p, :, c], v_ref[p, :, c], g_ref[p, :, c]
            weights = jnp.where(mask, mm(q, k, NT), 0.0).astype(jnp.bfloat16)
            diffs = jnp.where(mask, mm(g, v, NT), 0.0).astype(jnp.bfloat16)
            dq_ref[p, :, c] = (mm(diffs, k, NN) + mm(g, state_ref[p, i], NT)).astype(jnp.bfloat16)
            dk_ref[p, :, c] = mm(diffs, q, TN)
            dv_ref[p, :, c] = mm(weights, g, TN)


def final_body(k_ref, v_ref, dkp_ref, dvp_ref, own_ref, below_ref, above_ref, dk_ref, dv_ref):
    for i in range(k_ref.shape[2] // HEAD_DIM):
        c = head_cols(i)
        below = below_ref[i]
        laters = (below + own_ref[i] + above_ref[i], below)
        for p in range(2):
            later = laters[p].astype(jnp.bfloat16)
            k, v = k_ref[p, :, c], v_ref[p, :, c]
            dk_ref[p, :, c] = (dkp_ref[p, :, c] + mm(v, later, NT)).astype(jnp.bfloat16)
            dv_ref[p, :, c] = (dvp_ref[p, :, c] + mm(k, later, NN)).astype(jnp.bfloat16)


def project_body(slots, w_ref, hidden_ref, out_ref):
    for i, slot in enumerate(slots):
        out_ref[i] = mm(hidden_ref[...], w_ref[slot], NN).astype(out_ref.dtype)


def project(hidden, by_columns, slots, dtype):
    shape = (len(slots), hidden.shape[0], by_columns.shape[2])
    return kernel_call(functools.partial(project_body, slots), (shaped(shape, dtype),), (by_columns, hidden))[0]


def quarter_body(n, spot_ref, *refs):
    chunks, keep_ref, send_ref = refs[:n], refs[-2], refs[-1]
    seq, head = spot_ref[0], spot_ref[1]
    share, cols = keep_ref.shape[1:]
    rows = pl.ds(pl.multiple_of(head * share, share), share)
    odd = seq & 1
    for m in range(n):
        t = (seq // 2) ^ head ^ m
        entry = (t & 1) * (n // 2) + t // 2
        keep_ref[entry] = chunks[m][rows, pl.ds(pl.multiple_of(odd * cols, cols), cols)]
        send_ref[entry] = chunks[m][rows, pl.ds(pl.multiple_of((1 - odd) * cols, cols), cols)]


def columns_by_place(chunks, spot, waits):
    n = len(chunks)
    rows, cols = chunks[0].shape
    part = shaped((n, rows // n, cols // 2), chunks[0].dtype)
    keep, send = pl.pallas_call(
        functools.partial(quarter_body, n),
        out_shape=(part, part),
        in_specs=[pl.BlockSpec(memory_space=pltpu.SMEM)] + whole(n),
        out_specs=whole(2),
        compiler_params=pltpu.CompilerParams(vmem_limit_bytes=16 * 2**20),
        cost_estimate=lasting(0.5),
    )(spot, *chunks)
    got = xor_permute(send, "seq", 1)
    held = jnp.stack([keep, got], axis=1)
    bit = 1
    while bit < n:
        half = held.shape[0] // 2
        send = held[half:]
        if bit in waits:
            send = after(send, *waits[bit])
        got = xor_permute(send, "seq", 2 * bit)
        held = jnp.concatenate([held[:half], got], axis=1)
        bit *= 2
        if bit < n:
            held = jnp.concatenate([held[0::2], held[1::2]])
    return held[0]


def weight_body(slots, first, spot_ref, *refs):
    head = spot_ref[1]
    ups, out_ref = refs[len(slots)], refs[-1]
    n, _, share, _ = ups.shape
    lefts, rights = [], []
    for ref, group in zip(refs, slots):
        for i, slot in enumerate(group):
            for m in range(n):
                at = pl.multiple_of((head ^ m) * share, share)
                lefts.append(ref[i, pl.ds(at, share), :])
                rights.append(ups[m, slot])
    total = mm(jnp.concatenate(lefts), jnp.concatenate(rights), TN)
    out_ref[...] = total if first else refs[-2][...] + total


def weight_grad_of(hiddens, slots, ups, spot, before):
    features, cols = hiddens[0].shape[2], ups.shape[3]
    args = list(hiddens) + [ups] + ([] if before is None else [before])
    return pl.pallas_call(
        functools.partial(weight_body, slots, before is None),
        out_shape=shaped((features, cols), jnp.float32),
        in_specs=[pl.BlockSpec(memory_space=pltpu.SMEM)] + whole(len(args)),
        out_specs=pl.BlockSpec(memory_space=pltpu.VMEM),
        compiler_params=pltpu.CompilerParams(vmem_limit_bytes=16 * 2**20),
        cost_estimate=lasting(1),
    )(spot, *args)


def gather_xor(x, axis):
    held = {0: x}
    bit = lax.axis_size(axis) // 2
    while bit:
        for m in list(held):
            held[m ^ bit] = xor_permute(held[m], axis, bit)
        bit //= 2
    return [held[m] for m in range(len(held))]


def after(x, *others):
    return lax.optimization_barrier((x,) + others)[0]


def reduce_columns(away, home):
    got = xor_permute(away, "head", 1)
    total = home + got.astype(jnp.float32)
    bit = 2
    while bit < lax.axis_size("head"):
        total = total.reshape((-1, 2) + total.shape[1:])
        got = xor_permute(total[:, 1].astype(jnp.bfloat16), "head", bit)
        total = total[:, 0] + got.astype(jnp.float32)
        bit *= 2
    return total[0].astype(jnp.bfloat16)


def on_device(queries, keys, values, out_weight, upstream):
    pair, length, width = queries.shape
    heads = width // HEAD_DIM
    n_seq, n_head = lax.axis_size("seq"), lax.axis_size("head")
    seq, head = lax.axis_index("seq"), lax.axis_index("head")
    rows, own_cols = pair * length, upstream.shape[2]
    f32, bf16 = jnp.float32, jnp.bfloat16
    square = (heads, HEAD_DIM, HEAD_DIM)
    flat_up = upstream.reshape(rows, own_cols)
    spot = jnp.stack([seq, head]).astype(jnp.int32)
    split = n_seq == 2 * n_head

    kv_own, kv_send = kv_products(in_hbm(keys), in_hbm(values))
    sent_up = after(flat_up, kv_send)
    chunks = gather_xor(sent_up, "head")
    near_grad, by_columns, chunks[0] = near_grad_of(
        in_hbm(sent_up), in_hbm(out_weight), spot, n_head
    )
    hidden_grad = kernel_call(
        functools.partial(far_body, range(1, n_head)),
        (shaped((rows, width), f32),),
        [by_columns, near_grad] + chunks[1:],
        2,
    )[0]
    kv_rounds = Rounds(kv_own, kv_send, "seq", {})
    if split:
        ups = columns_by_place(chunks, spot, {1: (kv_rounds.sent[-1],)})

    states, hidden, attn_grad, qg_own, qg_send = kernel_call(
        forward_body,
        (
            shaped((2,) + square, bf16),
            shaped((rows, width), bf16),
            shaped((pair, length, width), bf16),
            shaped(square, f32),
            shaped((2,) + square, bf16),
        ),
        (queries, keys, values, hidden_grad, kv_own, kv_rounds.below, kv_rounds.above),
    )
    qg_rounds = Rounds(qg_own, qg_send, "seq", {})

    late = after(hidden, qg_rounds.sent[1])
    away = project(late, by_columns, range(1, n_head, 2), bf16)
    home = project(late, by_columns, range(0, n_head, 2), f32)
    output = reduce_columns(away, home)

    query_grad, key_part, value_part = kernel_call(
        inside_body,
        (
            shaped((pair, length, width), bf16),
            shaped((pair, length, width), f32),
            shaped((pair, length, width), f32),
        ),
        (queries, keys, values, after(attn_grad, qg_rounds.sent[1]), states),
        2,
    )
    key_grad, value_grad = kernel_call(
        final_body,
        (shaped((pair, length, width), bf16), shaped((pair, length, width), bf16)),
        (keys, values, key_part, value_part, qg_own, qg_rounds.below, qg_rounds.above),
    )

    if split:
        ups = jnp.stack(gather_xor(after(ups, qg_rounds.sent[1]), "head"))
        even = {0: hidden}
        bit = n_seq // 2
        while bit > 1:
            for m in list(even):
                block = even[m] if m == 0 else after(even[m], qg_rounds.sent[1])
                even[m ^ bit] = xor_permute(block, "seq", bit)
            bit //= 2
        order = [0, 2] + [m for m in range(4, n_seq, 2)]
        groups = [order[: n_seq // 4], order[n_seq // 4 :]]
        held, slots = [], []
        for i, group in enumerate(groups):
            block = after(jnp.stack([even[m] for m in group]), qg_rounds.sent[i + 1])
            held += [block, xor_permute(block, "seq", 1)]
            slots += [group, [m ^ 1 for m in group]]
        weight_grad = weight_grad_of(held[:3], slots[:3], ups, spot, None)
        weight_grad = weight_grad_of(held[3:], slots[3:], ups, spot, weight_grad)
    else:
        full_up = lax.all_gather(flat_up, "head", axis=1, tiled=True)
        weight_grad = lax.psum_scatter(
            mm(full_up, hidden, TN), "seq", scatter_dimension=0, tiled=True
        ).T

    return (
        output.reshape(pair, length, -1),
        query_grad,
        key_grad,
        value_grad,
        weight_grad,
    )


def solution(mesh):
    rows = P(None, "seq", "head")
    return jax.shard_map(
        on_device,
        mesh=mesh,
        in_specs=(rows, rows, rows, P("head", None), rows),
        out_specs=(rows, rows, rows, rows, P("head", "seq")),
        check_vma=False,
    )
```

```python
import functools

import jax
import jax.numpy as jnp
from jax import lax
from jax.experimental import pallas as pl
from jax.experimental.pallas import tpu as pltpu
from jax.sharding import PartitionSpec as P

HEAD_DIM = 128
EPS = 1e-06
CFG = {'x4': 1, 'got4_r3': 0, 'near_r2': 0, 'cost_inside': 1, 'inside': 1, 'quarter_r3': 1, 'wg': 1, 'rs_r3': 0, 'out_final': 1, 'a2_r1': 0, 'cost_wga': 2, 'final_wga': 0, 'project': 0, 'cost_stack': 0.5, 'out_wgb': 1, 'got4': 2, 'g3': 1, 'cost_kv': 5, 'cost_forward': 0.2, 'cost_final': 1, 'up4_late': 0, 'first_got': 0, 'got6_r3': 1, 'wga_final': 1, 'cost_join_kv': 0.01, 'cost_project': 0.2, 'first_r3': 1, 'quarter_far': 0, 'cost_wgb': 0.5, 'q_fwd': 1, 'gtrick': 0, 'got2': 1, 'q_when': 0}


def cfg(name, default=0):
    return CFG.get(name, default)

NN = (((1,), (0,)), ((), ()))
NT = (((1,), (1,)), ((), ()))
TN = (((0,), (0,)), ((), ()))


def mm(a, b, dims):
    return lax.dot_general(a, b, dims, preferred_element_type=jnp.float32)


def head_cols(i):
    return slice(i * HEAD_DIM, (i + 1) * HEAD_DIM)


def lower(length):
    rows = lax.broadcasted_iota(jnp.int32, (length, length), 0)
    cols = lax.broadcasted_iota(jnp.int32, (length, length), 1)
    return rows >= cols


def xor_permute(x, axis, bit):
    count = lax.axis_size(axis)
    return lax.ppermute(x, axis, [(i, i ^ bit) for i in range(count)])


def whole(n):
    return [pl.BlockSpec(memory_space=pltpu.VMEM)] * n


def lasting(name, us):
    us = cfg("cost_" + name, us)
    return pl.CostEstimate(flops=int(us * 1.1e9), bytes_accessed=0, transcendentals=0)


def kernel_call(name, body, outs, args, us=0.5, vmem=16 * 2**20):
    return pl.pallas_call(
        body,
        out_shape=outs,
        in_specs=whole(len(args)),
        out_specs=whole(len(outs)),
        compiler_params=pltpu.CompilerParams(vmem_limit_bytes=vmem),
        cost_estimate=lasting(name, us),
        name=name,
    )(*args)


def shaped(shape, dtype):
    return jax.ShapeDtypeStruct(shape, dtype)


def kv_body(k_hbm, v_hbm, own_ref, send_ref, k_ref, v_ref, sems):
    loads = [
        pltpu.make_async_copy(k_hbm, k_ref, sems.at[0]),
        pltpu.make_async_copy(v_hbm, v_ref, sems.at[1]),
    ]
    for load in loads:
        load.start()
    for load in loads:
        load.wait()
    for i in range(k_ref.shape[2] // HEAD_DIM):
        c = head_cols(i)
        first = mm(k_ref[0, :, c], v_ref[0, :, c], TN)
        second = mm(k_ref[1, :, c], v_ref[1, :, c], TN)
        own_ref[i] = first
        send_ref[0, i] = first.astype(jnp.bfloat16)
        send_ref[1, i] = (first + second).astype(jnp.bfloat16)


def in_hbm(x):
    return pltpu.with_memory_space_constraint(x, pltpu.HBM)


def kv_products(keys, values):
    heads = keys.shape[2] // HEAD_DIM
    square = (heads, HEAD_DIM, HEAD_DIM)
    return pl.pallas_call(
        kv_body,
        out_shape=(shaped(square, jnp.float32), shaped((2,) + square, jnp.bfloat16)),
        in_specs=[pl.BlockSpec(memory_space=pltpu.HBM)] * 2,
        out_specs=whole(2),
        scratch_shapes=[
            pltpu.VMEM(keys.shape, keys.dtype),
            pltpu.VMEM(values.shape, values.dtype),
            pltpu.SemaphoreType.DMA((2,)),
        ],
        compiler_params=pltpu.CompilerParams(vmem_limit_bytes=16 * 2**20),
    )(keys, values)


def join_body(a_ref, b_ref, out_ref):
    out_ref[...] = (a_ref[...].astype(jnp.float32) + b_ref[...].astype(jnp.float32)).astype(out_ref.dtype)


def swap_body(send_ref, q_ref, g_ref, next_ref, got_ref):
    for i in range(q_ref.shape[2] // HEAD_DIM):
        c = head_cols(i)
        first = mm(q_ref[0, :, c], g_ref[0, :, c], TN)
        second = mm(q_ref[1, :, c], g_ref[1, :, c], TN)
        for at, term in enumerate((second, first + second)):
            got_ref[at, i] = term.astype(jnp.bfloat16)
            next_ref[at, i] = (send_ref[at, i].astype(jnp.float32) + term).astype(jnp.bfloat16)


class Rounds:
    def __init__(self, name, near, send, axis, ahead, rounds=None, swap=None):
        self.name, self.swap = name, swap
        self.axis, self.rounds, self.bit = axis, rounds, 1
        self.below = jnp.zeros_like(near)
        self.above = jnp.zeros_like(near)
        self.next = send
        self.sent = []
        self.go_on(ahead)

    def go_on(self, ahead):
        count = lax.axis_size(self.axis)
        place = lax.axis_index(self.axis)
        while self.bit < count and len(self.sent) != self.rounds:
            bit, send = self.bit, self.next
            upper = (place & bit) != 0
            last = 2 * bit == count
            if last:
                send = jnp.where(upper, send[1], send[0])
            if bit in ahead:
                send = after(send, *ahead[bit])
            if bit == 1 and self.swap:
                theirs, mine = self.swap
                if bit in ahead:
                    mine = after(mine, *ahead[bit])
                self.sent.append(mine)
                got = xor_permute(mine, self.axis, bit)
                shape = shaped(send.shape, send.dtype)
                self.next, got = kernel_call("swap", swap_body, (shape, shape), (send, theirs, got))
            else:
                self.sent.append(send)
                got = xor_permute(send, self.axis, bit)
            if not last and not (bit == 1 and self.swap):
                self.next = kernel_call("join_" + self.name, join_body, (shaped(send.shape, send.dtype),), (send, got), 0.1)[0]
            got = got.astype(jnp.float32)
            got_near, got_both = (got, got) if last else (got[0], got[1])
            self.below = jnp.where(upper, self.below + got_near, self.below)
            self.above = jnp.where(upper, self.above, self.above + got_both)
            self.bit *= 2
        self.rounds = None


def pick(table, at):
    value = jnp.int32(table[0])
    for i, entry in enumerate(table[1:], 1):
        value = jnp.where(at == i, entry, value)
    return value


def near_body(spot_ref, w_hbm, up_hbm, out_ref, w_ref, up_ref, sems):
    n, _, cols = w_ref.shape
    loads = [pltpu.make_async_copy(up_hbm, up_ref, sems.at[n])]
    for slot in range(n):
        at = pl.multiple_of((spot_ref[1] ^ slot) * cols, cols)
        loads.append(pltpu.make_async_copy(w_hbm.at[:, pl.ds(at, cols)], w_ref.at[slot], sems.at[slot]))
    for load in loads:
        load.start()
    loads[0].wait()
    loads[1].wait()
    out_ref[...] = mm(up_ref[...], w_ref[0], NT)
    for load in loads[2:]:
        load.wait()


def near_grad_of(up, weight, spot, n):
    rows, cols = up.shape
    features = weight.shape[0]
    return pl.pallas_call(
        near_body,
        out_shape=(
            shaped((rows, features), jnp.float32),
            shaped((n, features, cols), weight.dtype),
            shaped(up.shape, up.dtype),
        ),
        in_specs=[pl.BlockSpec(memory_space=pltpu.SMEM)] + [pl.BlockSpec(memory_space=pltpu.HBM)] * 2,
        out_specs=whole(3),
        scratch_shapes=[pltpu.SemaphoreType.DMA((n + 1,))],
        compiler_params=pltpu.CompilerParams(vmem_limit_bytes=16 * 2**20),
        cost_estimate=lasting("near", 3),
        name="near",
    )(spot, weight, up)


def far_body(slots, w_ref, before_ref, *refs):
    chunks, out_ref = refs[:-1], refs[-1]
    total = before_ref[...]
    for i, slot in enumerate(slots):
        total += mm(chunks[i][...], w_ref[slot], NT)
    out_ref[...] = total


def forward_body(q_ref, k_ref, v_ref, hg_ref, own_ref, below_ref, above_ref,
                 state_ref, hidden_ref, g_ref, qown_ref, qsend_ref):
    length = q_ref.shape[1]
    mask = lower(length)
    for i in range(q_ref.shape[2] // HEAD_DIM):
        c = head_cols(i)
        below = below_ref[i]
        states = (below, below + own_ref[i] + above_ref[i])
        terms = []
        for p in range(2):
            r = slice(p * length, (p + 1) * length)
            q, k, v = q_ref[p, :, c], k_ref[p, :, c], v_ref[p, :, c]
            state = states[p].astype(jnp.bfloat16)
            state_ref[p, i] = state
            weights = jnp.where(mask, mm(q, k, NT), 0.0).astype(jnp.bfloat16)
            attended = mm(weights, v, NN) + mm(q, state, NN)
            scale = jnp.sqrt(jnp.mean(attended * attended, axis=-1, keepdims=True) + EPS)
            normed = attended / scale
            hidden_ref[r, c] = normed.astype(jnp.bfloat16)
            hg = hg_ref[r, c]
            inner = jnp.mean(hg * normed, axis=-1, keepdims=True)
            g = ((hg - normed * inner) / scale).astype(jnp.bfloat16)
            g_ref[p, :, c] = g
            terms.append(mm(q, g, TN))
        qown_ref[i] = terms[1]
        qsend_ref[0, i] = terms[1].astype(jnp.bfloat16)
        qsend_ref[1, i] = (terms[0] + terms[1]).astype(jnp.bfloat16)


def inside_body(q_ref, k_ref, v_ref, g_ref, state_ref, dq_ref, dk_ref, dv_ref):
    length = q_ref.shape[1]
    mask = lower(length)
    for i in range(q_ref.shape[2] // HEAD_DIM):
        c = head_cols(i)
        for p in range(2):
            q, k, v, g = q_ref[p, :, c], k_ref[p, :, c], v_ref[p, :, c], g_ref[p, :, c]
            weights = jnp.where(mask, mm(q, k, NT), 0.0).astype(jnp.bfloat16)
            diffs = jnp.where(mask, mm(g, v, NT), 0.0).astype(jnp.bfloat16)
            dq_ref[p, :, c] = (mm(diffs, k, NN) + mm(g, state_ref[p, i], NT)).astype(jnp.bfloat16)
            dk_ref[p, :, c] = mm(diffs, q, TN)
            dv_ref[p, :, c] = mm(weights, g, TN)


def final_body(k_ref, v_ref, dkp_ref, dvp_ref, own_ref, below_ref, above_ref, dk_ref, dv_ref):
    for i in range(k_ref.shape[2] // HEAD_DIM):
        c = head_cols(i)
        below = below_ref[i]
        laters = (below + own_ref[i] + above_ref[i], below)
        for p in range(2):
            later = laters[p].astype(jnp.bfloat16)
            k, v = k_ref[p, :, c], v_ref[p, :, c]
            dk_ref[p, :, c] = (dkp_ref[p, :, c] + mm(v, later, NT)).astype(jnp.bfloat16)
            dv_ref[p, :, c] = (dvp_ref[p, :, c] + mm(k, later, NN)).astype(jnp.bfloat16)


def project_body(slots, w_ref, hidden_ref, out_ref):
    for i, slot in enumerate(slots):
        out_ref[i] = mm(hidden_ref[...], w_ref[slot], NN).astype(out_ref.dtype)


def project(hidden, by_columns, slots, dtype):
    shape = (len(slots), hidden.shape[0], by_columns.shape[2])
    return kernel_call("project", functools.partial(project_body, slots), (shaped(shape, dtype),), (by_columns, hidden))[0]


def quarter_body(n, spot_ref, *refs):
    chunks, keep_ref, send_ref = refs[:n], refs[-2], refs[-1]
    seq, head = spot_ref[0], spot_ref[1]
    share, cols = keep_ref.shape[1:]
    rows = pl.ds(pl.multiple_of(head * share, share), share)
    odd = seq & 1
    for m in range(n):
        t = (seq // 2) ^ head ^ m
        entry = (t & 1) * (n // 2) + t // 2
        keep_ref[entry] = chunks[m][rows, pl.ds(pl.multiple_of(odd * cols, cols), cols)]
        send_ref[entry] = chunks[m][rows, pl.ds(pl.multiple_of((1 - odd) * cols, cols), cols)]


def share_out(chunks, spot):
    n = len(chunks)
    rows, cols = chunks[0].shape
    part = shaped((n, rows // n, cols // 2), chunks[0].dtype)
    return pl.pallas_call(
        functools.partial(quarter_body, n),
        out_shape=(part, part),
        in_specs=[pl.BlockSpec(memory_space=pltpu.SMEM)] + whole(n),
        out_specs=whole(2),
        compiler_params=pltpu.CompilerParams(vmem_limit_bytes=16 * 2**20),
        cost_estimate=lasting("quarter", 0.5),
        name="quarter",
    )(spot, *chunks)


def columns_by_place(keep, send):
    n = keep.shape[0]
    got = first_got = xor_permute(send, "seq", 1)
    held = jnp.stack([keep, got], axis=1)
    bit = 1
    while 2 * bit < n:
        half = held.shape[0] // 2
        got = xor_permute(held[half:], "seq", 2 * bit)
        held = jnp.concatenate([held[:half], got], axis=1)
        bit *= 2
        held = jnp.concatenate([held[0::2], held[1::2]])
    return held[0], held[1], got, first_got


def weight_body(slots, first, spot_ref, *refs):
    head = spot_ref[1]
    ups, out_ref = refs[len(slots)], refs[-1]
    n, _, share, _ = ups.shape
    lefts, rights = [], []
    for ref, group in zip(refs, slots):
        for i, slot in enumerate(group):
            for m in range(n):
                at = pl.multiple_of((head ^ m) * share, share)
                lefts.append(ref[i, pl.ds(at, share), :])
                rights.append(ups[m, slot])
    total = mm(jnp.concatenate(lefts), jnp.concatenate(rights), TN)
    out_ref[...] = total if first else refs[-2][...] + total


def weight_grad_of(name, hiddens, slots, ups, spot, before):
    features, cols = hiddens[0].shape[2], ups.shape[3]
    args = list(hiddens) + [ups] + ([] if before is None else [before])
    return pl.pallas_call(
        functools.partial(weight_body, slots, before is None),
        out_shape=shaped((features, cols), jnp.float32),
        in_specs=[pl.BlockSpec(memory_space=pltpu.SMEM)] + whole(len(args)),
        out_specs=pl.BlockSpec(memory_space=pltpu.VMEM),
        compiler_params=pltpu.CompilerParams(vmem_limit_bytes=16 * 2**20),
        cost_estimate=lasting(name, 1),
        name=name,
    )(spot, *args)


def gather_xor(x, axis):
    held = {0: x}
    bit = lax.axis_size(axis) // 2
    while bit:
        for m in list(held):
            held[m ^ bit] = xor_permute(held[m], axis, bit)
        bit //= 2
    return [held[m] for m in range(len(held))]


def gather_far(x, axis):
    held = {0: x}
    bit = lax.axis_size(axis) // 2
    while bit > 1:
        for m in list(held):
            held[m ^ bit] = xor_permute(held[m], axis, bit)
        bit //= 2
    return held


def stack_body(*refs):
    for i, ref in enumerate(refs[:-1]):
        refs[-1][i] = ref[...]


def stacked(blocks, us):
    shape = (len(blocks),) + blocks[0].shape
    return kernel_call("stack", stack_body, (shaped(shape, blocks[0].dtype),), blocks, us)[0]


def after(x, *others):
    if not others:
        return x
    return lax.optimization_barrier((x,) + others)[0]


class Columns:
    def __init__(self, away, home):
        self.got = xor_permute(away, "head", 1)
        self.total = home + self.got.astype(jnp.float32)
        self.bit = 2
        self.split()

    def split(self):
        self.send = None
        if self.bit < lax.axis_size("head"):
            total = self.total.reshape((-1, 2) + self.total.shape[1:])
            self.total, self.send = total[:, 0], total[:, 1].astype(jnp.bfloat16)

    def finish(self):
        while self.send is not None:
            got = xor_permute(self.send, "head", self.bit)
            self.total = self.total + got.astype(jnp.float32)
            self.bit *= 2
            self.split()
        return self.total[0].astype(jnp.bfloat16)


def on_device(queries, keys, values, out_weight, upstream):
    pair, length, width = queries.shape
    heads = width // HEAD_DIM
    n_seq, n_head = lax.axis_size("seq"), lax.axis_size("head")
    seq, head = lax.axis_index("seq"), lax.axis_index("head")
    rows, own_cols = pair * length, upstream.shape[2]
    f32, bf16 = jnp.float32, jnp.bfloat16
    square = (heads, HEAD_DIM, HEAD_DIM)
    flat_up = upstream.reshape(rows, own_cols)
    spot = jnp.stack([seq, head]).astype(jnp.int32)
    split = n_seq == 8 and n_head == 4

    kv_own, kv_send = kv_products(in_hbm(keys), in_hbm(values))
    sent_up = after(flat_up, kv_send)
    chunks = gather_xor(sent_up, "head")
    near_grad, by_columns, chunks[0] = near_grad_of(
        in_hbm(sent_up), in_hbm(out_weight), spot, n_head
    )
    far_before = near_grad
    if split:
        shares = share_out(chunks, spot)
        if cfg("quarter_far"):
            far_before = after(near_grad, shares[1])
    hidden_grad = kernel_call(
        "far",
        functools.partial(far_body, range(1, n_head)),
        (shaped((rows, width), f32),),
        [by_columns, far_before] + chunks[1:],
        2,
    )[0]
    ahead = {}
    if cfg("near_r2", 1):
        ahead[2] = (near_grad,)
    if split and cfg("quarter_r3"):
        ahead[n_seq // 2] = (shares[1],)
    kv_rounds = Rounds("kv", kv_own, kv_send, "seq", ahead)
    kv_below = kv_rounds.below
    if cfg("gtrick"):
        due_after = [kv_send, kv_rounds.sent[1], kv_rounds.sent[2]][cfg("q_when", 1)]
        their_queries = xor_permute(after(queries, due_after), "seq", 1)
        if cfg("q_fwd"):
            kv_below = after(kv_below, their_queries)
    ahead = {1: (), 2: (), 4: ()}
    if split:
        ups_keep, ups_send, ups_got, ups_got1 = columns_by_place(*shares)
        kv_below = after(kv_below, *[(), (ups_got1,), (ups_got,)][cfg("fwd_a", 0)])
        if cfg("a2_r1"):
            ahead[1] = (ups_got,)

    states, hidden, attn_grad, qg_own, qg_send = kernel_call(
        "forward",
        forward_body,
        (
            shaped((2,) + square, bf16),
            shaped((rows, width), bf16),
            shaped((pair, length, width), bf16),
            shaped(square, f32),
            shaped((2,) + square, bf16),
        ),
        (queries, keys, values, hidden_grad, kv_own, kv_below, kv_rounds.above),
    )

    def due(x, rule):
        return x if rule == 0 else after(x, qg_rounds.sent[rule])

    even = {0: hidden}
    if split:
        if cfg("x4", 1):
            across = jnp.stack([hidden, ups_send.reshape(hidden.shape)])
            across = xor_permute(across, "seq", n_seq // 2)
            got4, got_up = across[0], across[1].reshape(ups_keep.shape)
        else:
            got4 = xor_permute(hidden, "seq", n_seq // 2)
            got_up = xor_permute(ups_send, "seq", n_seq // 2)
        got2 = xor_permute(hidden, "seq", 2)
        if cfg("got2_r2"):
            ahead[2] += (got2,)
        if cfg("up4_r2"):
            ahead[2] += (got_up,)
    swap = (their_queries, attn_grad) if cfg("gtrick") else None
    qg_rounds = Rounds("qg", qg_own, qg_send, "seq", ahead, 2, swap)

    late = due(hidden, cfg("project", 1))
    away = project(late, by_columns, range(1, n_head, 2), bf16)
    home = project(late, by_columns, range(0, n_head, 2), f32)
    sums = Columns(away, home)
    ahead = ()
    if cfg("rs_r3", 1):
        ahead += (sums.got,)
    if split:
        even[2] = due(got2, cfg("got2", 1))
        if not cfg("up4_late"):
            ups = jnp.concatenate([ups_keep, due(got_up, cfg("up4", 1))])
            ups = gather_far(ups, "head")
            if cfg("g_r3"):
                ahead += (ups[2],)
        first_rows = stacked([hidden, even[2]], 0.1)
        first_got = xor_permute(first_rows, "seq", 1)
        if cfg("first_r3"):
            ahead += (first_got,)
        if cfg("h6", 0) == 0:
            got6 = xor_permute(even[2], "seq", n_seq // 2)
        if cfg("got4_r3"):
            ahead += (got4,)
        if cfg("got6_r3") and cfg("h6", 0) == 0:
            ahead += (got6,)
    qg_rounds.go_on({n_seq // 2: ahead})
    third = qg_rounds.sent[2]
    if split:
        even[4] = due(got4, cfg("got4", 2))
        if cfg("h6", 0):
            got6 = xor_permute(even[4], "seq", 2)
        even[6] = due(got6, cfg("got6", 2))
        second_rows = stacked([even[4], even[6]], 0.1)
        second_got = xor_permute(second_rows, "seq", 1)
        if cfg("up4_late"):
            ups = jnp.concatenate([ups_keep, after(got_up, third)])
            ups = gather_far(ups, "head")
        ups[1] = xor_permute(due(ups[0], cfg("g1", 0)), "head", 1)
        ups[3] = xor_permute(due(ups[2], cfg("g3", 2)), "head", 1)
        ups = jnp.stack([ups[m] for m in range(n_head)])
        first_got = due(first_got, cfg("first_got", 2))
    output = sums.finish()

    query_grad, key_part, value_part = kernel_call(
        "inside",
        inside_body,
        (
            shaped((pair, length, width), bf16),
            shaped((pair, length, width), f32),
            shaped((pair, length, width), f32),
        ),
        (queries, keys, values, due(attn_grad, cfg("inside", 1)), states),
        2,
    )
    if cfg("out_final"):
        key_part = after(key_part, output)
    if split:
        if cfg("wg", 0) == 0:
            weight_part = weight_grad_of("wga", [first_rows, first_got], [[0, 2], [1, 3]], ups, spot, None)
            if cfg("wga_final"):
                key_part = after(key_part, weight_part)
    key_grad, value_grad = kernel_call(
        "final",
        final_body,
        (shaped((pair, length, width), bf16), shaped((pair, length, width), bf16)),
        (keys, values, key_part, value_part, qg_own, qg_rounds.below, qg_rounds.above),
    )
    if split:
        if cfg("wg", 0) == 0:
            deps = [key_grad] + ([output] if cfg("out_wgb", 1) else [])
            if cfg("final_wga"):
                weight_part = after(weight_part, *deps)
                second_got = after(second_got, weight_part)
            else:
                second_got = after(second_got, *deps)
            weight_grad = weight_grad_of("wgb", [second_rows, second_got], [[4, 6], [5, 7]], ups, spot, weight_part)
        else:
            second_got = after(second_got, key_grad)
            weight_grad = weight_grad_of(
                "wgb", [first_rows, first_got, second_rows, second_got], [[0, 2], [1, 3], [4, 6], [5, 7]], ups, spot, None
            )
    else:
        full_up = lax.all_gather(flat_up, "head", axis=1, tiled=True)
        weight_grad = lax.psum_scatter(
            mm(full_up, hidden, TN), "seq", scatter_dimension=0, tiled=True
        ).T

    return (
        output.reshape(pair, length, -1),
        query_grad,
        key_grad,
        value_grad,
        weight_grad,
    )


def solution(mesh):
    rows = P(None, "seq", "head")
    return jax.shard_map(
        on_device,
        mesh=mesh,
        in_specs=(rows, rows, rows, P("head", None), rows),
        out_specs=(rows, rows, rows, rows, P("head", "seq")),
        check_vma=False,
    )
```

```python
import functools

import jax
import jax.numpy as jnp
from jax import lax
from jax.experimental import pallas as pl
from jax.experimental.pallas import tpu as pltpu
from jax.sharding import PartitionSpec as P

HEAD_DIM = 128
EPS = 1e-06
LASTING = {
    "kv": 3,
    "near": 3,
    "quarter": 0.2,
    "far": 0.01,
    "forward": 0.01,
    "join_kv": 0.01,
    "join_qg": 0.1,
    "project": 0.2,
    "inside": 5,
    "stack": 0.1,
    "last": 1,
}
WAITS = {
    "kv4.s": ["quarter", "a1.s", "near"],
    "h2.s": ["far", "a1.g"],
    "rs2.s": ["a2.s"],
    "a4.g": ["qg2.s", "qg1.g"],
    "g1.g": ["hy.g"],
    "qg4.g": ["h2.g", "rs2.g"],
    "h6.g": ["qg2.s"],
    "qg1.s": ["a2.g", "kv2.s"],
    "away": ["c2.g"],
    "qg4.s": ["rs2.s", "a4.s", "g1.s"],
    "hy.s": ["c3.g"],
    "forward": ["a1.g"],
    "qg2.s": ["a2.g"],
    "a2.s": ["c1.s"],
    "quarter": ["kv1.s"],
    "kv1.g": ["c1.s"],
    "g3.g": ["qg4.g"],
    "hz.g": ["qg4.g"],
    "c1.s": ["c2.s"],
    "c2.s": ["kv1.s"],
    "hz.s": ["rs2.s", "h4.g"],
    "qg2.g": ["g1.s"],
    "g1.s": ["h6.g"],
}

NN = (((1,), (0,)), ((), ()))
NT = (((1,), (1,)), ((), ()))
TN = (((0,), (0,)), ((), ()))


def mm(a, b, dims):
    return lax.dot_general(a, b, dims, preferred_element_type=jnp.float32)


def head_cols(i):
    return slice(i * HEAD_DIM, (i + 1) * HEAD_DIM)


def lower(length):
    rows = lax.broadcasted_iota(jnp.int32, (length, length), 0)
    cols = lax.broadcasted_iota(jnp.int32, (length, length), 1)
    return rows >= cols


def xor_permute(x, axis, bit):
    count = lax.axis_size(axis)
    return lax.ppermute(x, axis, [(i, i ^ bit) for i in range(count)])


def whole(n):
    return [pl.BlockSpec(memory_space=pltpu.VMEM)] * n


def lasting(name):
    return pl.CostEstimate(flops=int(LASTING[name] * 1.1e9), bytes_accessed=0, transcendentals=0)


def kernel_call(name, body, outs, args, vmem=16 * 2**20):
    return pl.pallas_call(
        body,
        out_shape=outs,
        in_specs=whole(len(args)),
        out_specs=whole(len(outs)),
        compiler_params=pltpu.CompilerParams(vmem_limit_bytes=vmem),
        cost_estimate=lasting(name),
        name=name,
    )(*args)


def shaped(shape, dtype):
    return jax.ShapeDtypeStruct(shape, dtype)


def kv_body(k_hbm, v_hbm, own_ref, send_ref, k_ref, v_ref, sems):
    loads = [
        pltpu.make_async_copy(k_hbm, k_ref, sems.at[0]),
        pltpu.make_async_copy(v_hbm, v_ref, sems.at[1]),
    ]
    for load in loads:
        load.start()
    for load in loads:
        load.wait()
    for i in range(k_ref.shape[2] // HEAD_DIM):
        c = head_cols(i)
        first = mm(k_ref[0, :, c], v_ref[0, :, c], TN)
        second = mm(k_ref[1, :, c], v_ref[1, :, c], TN)
        own_ref[i] = first
        send_ref[0, i] = first.astype(jnp.bfloat16)
        send_ref[1, i] = (first + second).astype(jnp.bfloat16)


def in_hbm(x):
    return pltpu.with_memory_space_constraint(x, pltpu.HBM)


def kv_products(keys, values):
    heads = keys.shape[2] // HEAD_DIM
    square = (heads, HEAD_DIM, HEAD_DIM)
    return pl.pallas_call(
        kv_body,
        out_shape=(shaped(square, jnp.float32), shaped((2,) + square, jnp.bfloat16)),
        in_specs=[pl.BlockSpec(memory_space=pltpu.HBM)] * 2,
        out_specs=whole(2),
        scratch_shapes=[
            pltpu.VMEM(keys.shape, keys.dtype),
            pltpu.VMEM(values.shape, values.dtype),
            pltpu.SemaphoreType.DMA((2,)),
        ],
        compiler_params=pltpu.CompilerParams(vmem_limit_bytes=16 * 2**20),
    )(keys, values)


def join_body(a_ref, b_ref, out_ref):
    out_ref[...] = (a_ref[...].astype(jnp.float32) + b_ref[...].astype(jnp.float32)).astype(out_ref.dtype)


def column_loads(spot_ref, w_hbm, w_ref, sems):
    n, _, cols = w_ref.shape
    loads = []
    for slot in range(n):
        at = pl.multiple_of((spot_ref[1] ^ slot) * cols, cols)
        loads.append(pltpu.make_async_copy(w_hbm.at[:, pl.ds(at, cols)], w_ref.at[slot], sems.at[slot]))
    return loads


def near_body(spot_ref, w_hbm, up_hbm, out_ref, up_ref, w_ref, sems):
    loads = [pltpu.make_async_copy(up_hbm, up_ref, sems.at[1])] + column_loads(spot_ref, w_hbm, w_ref, sems)
    for load in loads:
        load.start()
    for load in loads:
        load.wait()
    out_ref[...] = mm(up_ref[...], w_ref[0], NT)


def near_grad_of(up, weight, spot):
    rows, cols = up.shape
    features = weight.shape[0]
    return pl.pallas_call(
        near_body,
        out_shape=(shaped((rows, features), jnp.float32), shaped(up.shape, up.dtype)),
        in_specs=[pl.BlockSpec(memory_space=pltpu.SMEM)] + [pl.BlockSpec(memory_space=pltpu.HBM)] * 2,
        out_specs=whole(2),
        scratch_shapes=[pltpu.VMEM((1, features, cols), weight.dtype), pltpu.SemaphoreType.DMA((2,))],
        compiler_params=pltpu.CompilerParams(vmem_limit_bytes=16 * 2**20),
        cost_estimate=lasting("near"),
        name="near",
    )(spot, weight, up)


def far_body(n, spot_ref, w_hbm, before_ref, *refs):
    chunks, (out_ref, w_ref, sems) = refs[: n - 1], refs[n - 1 :]
    loads = column_loads(spot_ref, w_hbm, w_ref, sems)
    for load in loads[1:] + loads[:1]:
        load.start()
    total = before_ref[...]
    for slot in range(1, n):
        loads[slot].wait()
        total += mm(chunks[slot - 1][...], w_ref[slot], NT)
    out_ref[...] = total
    loads[0].wait()


def hidden_grad_of(before, chunks, weight, spot):
    rows, cols = chunks[0].shape
    features = weight.shape[0]
    n = len(chunks) + 1
    return pl.pallas_call(
        functools.partial(far_body, n),
        out_shape=(shaped((rows, features), jnp.float32), shaped((n, features, cols), weight.dtype)),
        in_specs=[pl.BlockSpec(memory_space=pltpu.SMEM), pl.BlockSpec(memory_space=pltpu.HBM)] + whole(n),
        out_specs=whole(2),
        scratch_shapes=[pltpu.SemaphoreType.DMA((n,))],
        compiler_params=pltpu.CompilerParams(vmem_limit_bytes=16 * 2**20),
        cost_estimate=lasting("far"),
        name="far",
    )(spot, weight, before, *chunks)


def forward_body(q_ref, k_ref, v_ref, hg_ref, own_ref, below_ref, above_ref,
                 state_ref, hidden_ref, g_ref, qown_ref, qsend_ref):
    length = q_ref.shape[1]
    mask = lower(length)
    for i in range(q_ref.shape[2] // HEAD_DIM):
        c = head_cols(i)
        below = below_ref[i]
        states = (below, below + own_ref[i] + above_ref[i])
        terms = []
        for p in range(2):
            r = slice(p * length, (p + 1) * length)
            q, k, v = q_ref[p, :, c], k_ref[p, :, c], v_ref[p, :, c]
            state = states[p].astype(jnp.bfloat16)
            state_ref[p, i] = state
            weights = jnp.where(mask, mm(q, k, NT), 0.0).astype(jnp.bfloat16)
            attended = mm(weights, v, NN) + mm(q, state, NN)
            scale = jnp.sqrt(jnp.mean(attended * attended, axis=-1, keepdims=True) + EPS)
            normed = attended / scale
            hidden_ref[r, c] = normed.astype(jnp.bfloat16)
            hg = hg_ref[r, c]
            inner = jnp.mean(hg * normed, axis=-1, keepdims=True)
            g = ((hg - normed * inner) / scale).astype(jnp.bfloat16)
            g_ref[p, :, c] = g
            terms.append(mm(q, g, TN))
        qown_ref[i] = terms[1]
        qsend_ref[0, i] = terms[1].astype(jnp.bfloat16)
        qsend_ref[1, i] = (terms[0] + terms[1]).astype(jnp.bfloat16)


def inside_body(q_ref, k_ref, v_ref, g_ref, state_ref, dq_ref, dk_ref, dv_ref):
    length = q_ref.shape[1]
    mask = lower(length)
    for i in range(q_ref.shape[2] // HEAD_DIM):
        c = head_cols(i)
        for p in range(2):
            q, k, v, g = q_ref[p, :, c], k_ref[p, :, c], v_ref[p, :, c], g_ref[p, :, c]
            weights = jnp.where(mask, mm(q, k, NT), 0.0).astype(jnp.bfloat16)
            diffs = jnp.where(mask, mm(g, v, NT), 0.0).astype(jnp.bfloat16)
            dq_ref[p, :, c] = (mm(diffs, k, NN) + mm(g, state_ref[p, i], NT)).astype(jnp.bfloat16)
            dk_ref[p, :, c] = mm(diffs, q, TN)
            dv_ref[p, :, c] = mm(weights, g, TN)


def last_body(slots, spot_ref, k_ref, v_ref, dkp_ref, dvp_ref, own_ref, below_ref, above_ref, sum_ref, got_ref, *refs):
    hiddens, ups = refs[: len(slots)], refs[len(slots)]
    outs, sems = refs[len(slots) + 1 : len(slots) + 5], refs[-1]
    dk_ref, dv_ref, out_ref, weight_ref = refs[len(slots) + 5 : -1]
    features = weight_ref.shape[0]
    tile = features // 2
    copies = [pltpu.make_async_copy(x, y, sems.at[i]) for i, (x, y) in enumerate(zip((dk_ref, dv_ref, out_ref), outs))]
    copies += [
        pltpu.make_async_copy(weight_ref.at[pl.ds(t * tile, tile)], outs[3].at[pl.ds(t * tile, tile)], sems.at[3 + t])
        for t in range(2)
    ]
    out_ref[...] = (sum_ref[...] + got_ref[...].astype(jnp.float32)).astype(out_ref.dtype)
    copies[2].start()
    for i in range(k_ref.shape[2] // HEAD_DIM):
        c = head_cols(i)
        below = below_ref[i]
        laters = (below + own_ref[i] + above_ref[i], below)
        for p in range(2):
            later = laters[p].astype(jnp.bfloat16)
            k, v = k_ref[p, :, c], v_ref[p, :, c]
            dk_ref[p, :, c] = (dkp_ref[p, :, c] + mm(v, later, NT)).astype(jnp.bfloat16)
            dv_ref[p, :, c] = (dvp_ref[p, :, c] + mm(k, later, NN)).astype(jnp.bfloat16)
    copies[0].start()
    copies[1].start()
    head = spot_ref[1]
    n, _, share, _ = ups.shape
    rights = jnp.concatenate([ups[m, slot] for group in slots for slot in group for m in range(n)])
    for t in range(2):
        lefts = [
            ref[i, pl.ds(pl.multiple_of((head ^ m) * share, share), share), t * tile : (t + 1) * tile]
            for ref, group in zip(hiddens, slots)
            for i in range(len(group))
            for m in range(n)
        ]
        weight_ref[t * tile : (t + 1) * tile, :] = mm(jnp.concatenate(lefts), rights, TN)
        copies[3 + t].start()
    for copy in copies:
        copy.wait()


def last_call(slots, shapes, spot, args):
    n = len(args)
    return pl.pallas_call(
        functools.partial(last_body, slots),
        out_shape=shapes,
        in_specs=[pl.BlockSpec(memory_space=pltpu.SMEM)] + whole(n),
        out_specs=[pl.BlockSpec(memory_space=pl.ANY)] * len(shapes),
        scratch_shapes=[pltpu.VMEM(x.shape, x.dtype) for x in shapes] + [pltpu.SemaphoreType.DMA((5,))],
        compiler_params=pltpu.CompilerParams(vmem_limit_bytes=24 * 2**20),
        cost_estimate=lasting("last"),
        name="last",
    )(spot, *args)


def project_body(slots, w_ref, hidden_ref, out_ref):
    for i, slot in enumerate(slots):
        out_ref[i] = mm(hidden_ref[...], w_ref[slot], NN).astype(out_ref.dtype)


def project(hidden, by_columns, slots, dtype):
    shape = (len(slots), hidden.shape[0], by_columns.shape[2])
    return kernel_call("project", functools.partial(project_body, slots), (shaped(shape, dtype),), (by_columns, hidden))[0]


def quarter_body(n, spot_ref, *refs):
    chunks, keep_ref, send_ref = refs[:n], refs[-2], refs[-1]
    seq, head = spot_ref[0], spot_ref[1]
    share, cols = keep_ref.shape[1:]
    rows = pl.ds(pl.multiple_of(head * share, share), share)
    odd = seq & 1
    for m in range(n):
        t = (seq // 2) ^ head ^ m
        entry = (t & 1) * (n // 2) + t // 2
        keep_ref[entry] = chunks[m][rows, pl.ds(pl.multiple_of(odd * cols, cols), cols)]
        send_ref[entry] = chunks[m][rows, pl.ds(pl.multiple_of((1 - odd) * cols, cols), cols)]


def share_out(chunks, spot):
    n = len(chunks)
    rows, cols = chunks[0].shape
    part = shaped((n, rows // n, cols // 2), chunks[0].dtype)
    return pl.pallas_call(
        functools.partial(quarter_body, n),
        out_shape=(part, part),
        in_specs=[pl.BlockSpec(memory_space=pltpu.SMEM)] + whole(n),
        out_specs=whole(2),
        compiler_params=pltpu.CompilerParams(vmem_limit_bytes=16 * 2**20),
        cost_estimate=lasting("quarter"),
        name="quarter",
    )(spot, *chunks)


def stack_body(*refs):
    for i, ref in enumerate(refs[:-1]):
        refs[-1][i] = ref[...]


def stacked(blocks):
    shape = (len(blocks),) + blocks[0].shape
    return kernel_call("stack", stack_body, (shaped(shape, blocks[0].dtype),), blocks)[0]


def after(x, *others):
    if not others:
        return x
    return lax.optimization_barrier((x,) + others)[0]


def on_eight_by_four(queries, keys, values, out_weight, upstream):
    pair, length, width = queries.shape
    heads = width // HEAD_DIM
    n_seq, n_head = lax.axis_size("seq"), lax.axis_size("head")
    seq, head = lax.axis_index("seq"), lax.axis_index("head")
    rows, own_cols = pair * length, upstream.shape[2]
    f32, bf16 = jnp.float32, jnp.bfloat16
    square = (heads, HEAD_DIM, HEAD_DIM)
    flat_up = upstream.reshape(rows, own_cols)
    spot = jnp.stack([seq, head]).astype(jnp.int32)
    seen = {}

    def node(name, x):
        early = [seen[other] for other in WAITS.get(name, ()) if other in seen]
        if early:
            x = after(x, *early)
        seen[name] = x
        return x

    class Scan:
        def __init__(self, tag, near, send):
            self.tag, self.send = tag, send
            self.below = jnp.zeros_like(near)
            self.above = jnp.zeros_like(near)

        def put(self, bit):
            self.upper = (seq & bit) != 0
            if 2 * bit == n_seq:
                self.send = jnp.where(self.upper, self.send[1], self.send[0])
            self.name = self.tag + str(bit)
            self.send = node(self.name + ".s", self.send)
            self.raw = xor_permute(self.send, "seq", bit)

        def take(self):
            got = node(self.name + ".g", self.raw)
            if got.ndim == 4:
                self.send = kernel_call("join_" + self.tag, join_body, (shaped(got.shape, got.dtype),), (self.send, got))[0]
            self.add(got.astype(jnp.float32))

        def add(self, got):
            near, both = (got[0], got[1]) if got.ndim == 4 else (got, got)
            self.below = jnp.where(self.upper, self.below + near, self.below)
            self.above = jnp.where(self.upper, self.above, self.above + both)

    kv_own, kv_send = kv_products(in_hbm(keys), in_hbm(values))
    kv = Scan("kv", kv_own, kv_send)
    kv.put(1)
    seen["kv"] = kv_send
    flat_up = after(flat_up, kv_send)
    c2_raw = xor_permute(node("c2.s", flat_up), "head", 2)
    c1_raw = xor_permute(node("c1.s", flat_up), "head", 1)
    weight_hbm = in_hbm(out_weight)
    near_grad, c0 = near_grad_of(in_hbm(node("near", flat_up)), weight_hbm, spot)
    near_grad = node("near_out", near_grad)
    kv.take()
    kv.put(2)
    c2 = node("c2.g", c2_raw)
    c3_raw = xor_permute(node("c3.s", c2), "head", 1)
    c1 = node("c1.g", c1_raw)
    c3 = node("c3.g", c3_raw)
    chunks = [c0, c1, c2, c3]
    keep, a1_send = share_out([node("quarter", c0)] + chunks[1:], spot)
    a1_raw = xor_permute(node("a1.s", a1_send), "seq", 1)
    kv.take()
    kv.put(4)
    a1 = node("a1.g", a1_raw)
    held = jnp.stack([keep, a1], axis=1)
    a2_raw = xor_permute(node("a2.s", held[2:]), "seq", 2)
    hidden_grad, by_columns = hidden_grad_of(node("far", near_grad), chunks[1:], weight_hbm, spot)
    a2 = node("a2.g", a2_raw)
    held = jnp.concatenate([held[:2], a2], axis=1)
    a4_raw = xor_permute(node("a4.s", held[1]), "seq", 4)
    kv.take()
    states, hidden, attn_grad, qg_own, qg_send = kernel_call(
        "forward",
        forward_body,
        (
            shaped((2,) + square, bf16),
            shaped((rows, width), bf16),
            shaped((pair, length, width), bf16),
            shaped(square, f32),
            shaped((2,) + square, bf16),
        ),
        (queries, keys, values, node("forward", hidden_grad), kv_own, kv.below, kv.above),
    )
    qg = Scan("qg", qg_own, qg_send)
    qg.put(1)
    h2_raw = xor_permute(node("h2.s", hidden), "seq", 2)
    h4_raw = xor_permute(node("h4.s", hidden), "seq", 4)
    away = project(node("away", hidden), by_columns, range(1, n_head, 2), bf16)
    rs1_raw = xor_permute(node("rs1.s", away), "head", 1)
    home = project(node("home", hidden), by_columns, range(0, n_head, 2), f32)
    qg.take()
    qg.put(2)
    h2 = node("h2.g", h2_raw)
    first_rows = stacked([hidden, h2])
    hy_raw = xor_permute(node("hy.s", first_rows), "seq", 1)
    rs1 = node("rs1.g", rs1_raw)
    total = (home + rs1.astype(f32)).reshape(2, rows, own_cols)
    rs2_raw = xor_permute(node("rs2.s", total[1].astype(bf16)), "head", 2)

    query_grad, key_part, value_part = kernel_call(
        "inside",
        inside_body,
        (
            shaped((pair, length, width), bf16),
            shaped((pair, length, width), f32),
            shaped((pair, length, width), f32),
        ),
        (queries, keys, values, node("inside", attn_grad), states),
    )
    ups = jnp.concatenate([held[0], node("a4.g", a4_raw)])
    h4 = node("h4.g", h4_raw)
    g2_raw = xor_permute(node("g2.s", ups), "head", 2)
    h6_raw = xor_permute(node("h6.s", h4), "seq", 2)
    h6 = node("h6.g", h6_raw)
    second_rows = stacked([h4, h6])
    hz_raw = xor_permute(node("hz.s", second_rows), "seq", 1)
    g1_raw = xor_permute(node("g1.s", ups), "head", 1)
    qg.take()
    qg.put(4)
    g2 = node("g2.g", g2_raw)
    g3_raw = xor_permute(node("g3.s", g2), "head", 1)
    hy = node("hy.g", hy_raw)
    g1 = node("g1.g", g1_raw)
    rs2 = node("rs2.g", rs2_raw)
    qg.take()
    hz = node("hz.g", hz_raw)
    g3 = node("g3.g", g3_raw)
    ups = jnp.stack([ups, g1, g2, g3])
    key_grad, value_grad, output, weight_grad = last_call(
        [[0, 2], [1, 3], [4, 6], [5, 7]],
        (
            shaped((pair, length, width), bf16),
            shaped((pair, length, width), bf16),
            shaped((rows, own_cols), bf16),
            shaped((width, own_cols // 2), f32),
        ),
        spot,
        [keys, values, node("final", key_part), value_part, qg_own, qg.below, qg.above, total[0], rs2]
        + [first_rows, hy, second_rows, hz, ups],
    )
    return (
        output.reshape(pair, length, -1),
        query_grad,
        key_grad,
        value_grad,
        weight_grad,
    )


def carried_in(shard, axis, join, neutral, backward):
    count = lax.axis_size(axis)
    place = lax.axis_index(axis)
    ahead = count - 1 - place if backward else place
    gathered = lax.all_gather(shard.astype(jnp.bfloat16), axis)
    state = jnp.zeros_like(shard) + jnp.asarray(neutral, shard.dtype)

    def one(lap, state):
        source = count - 1 - lap if backward else lap
        return join(state, lax.dynamic_index_in_dim(gathered, source, 0, False).astype(shard.dtype))

    return lax.fori_loop(0, ahead, one, state)


def add_terms(earlier, later):
    return jax.tree.map(lambda left, right: left + right, earlier, later)


def on_any_mesh(queries, keys, values, out_weight, upstream):
    pair, length, width = queries.shape
    heads_here = width // HEAD_DIM
    shape_four = (pair, length, heads_here, HEAD_DIM)
    query4 = queries.reshape(shape_four)
    key4 = keys.reshape(shape_four)
    value4 = values.reshape(shape_four)
    kv_terms = jnp.einsum("pchd,pche->phde", key4, value4, preferred_element_type=jnp.float32)
    first_kv = kv_terms[0]
    second_kv = kv_terms[1]
    zero_state = jnp.zeros_like(first_kv)
    before = carried_in(first_kv, "seq", add_terms, zero_state, False)
    after = carried_in(second_kv, "seq", add_terms, zero_state, True)
    total_first = lax.psum(first_kv, "seq")
    state_second = total_first + after
    states = jnp.stack([before, state_second]).astype(jnp.bfloat16)
    mask = lower(length)
    scores = jnp.einsum("pthd,pshd->phts", query4, key4, preferred_element_type=jnp.float32)
    weights = jnp.where(mask, scores, 0.0).astype(jnp.bfloat16)
    attended = jnp.einsum("phts,pshe->pthe", weights, value4, preferred_element_type=jnp.float32)
    attended = attended + jnp.einsum(
        "pthd,phde->pthe", query4, states, preferred_element_type=jnp.float32
    )
    scale = jnp.sqrt(jnp.mean(attended * attended, axis=-1, keepdims=True) + EPS)
    normed = attended / scale
    hidden = normed.astype(jnp.bfloat16).reshape(pair * length, width)
    partial_out = jnp.dot(hidden, out_weight, preferred_element_type=jnp.float32)
    output = lax.psum_scatter(
        partial_out.astype(jnp.bfloat16), "head", scatter_dimension=1, tiled=True
    ).astype(jnp.float32)
    output = output.astype(jnp.bfloat16).reshape(pair, length, -1)
    flat_up = upstream.reshape(pair * length, upstream.shape[2])
    full_up = lax.all_gather(flat_up, "head", axis=1, tiled=True)
    hidden_grad = lax.dot_general(
        full_up, out_weight, (((1,), (1,)), ((), ())), preferred_element_type=jnp.float32
    )
    weight_share = lax.psum_scatter(
        lax.dot_general(
            full_up, hidden, (((0,), (0,)), ((), ())), preferred_element_type=jnp.float32
        ),
        "seq",
        scatter_dimension=0,
        tiled=True,
    )
    weight_grad = weight_share.T
    grad_four = hidden_grad.reshape(shape_four)
    inner = jnp.mean(grad_four * normed, axis=-1, keepdims=True)
    attn_grad = ((grad_four - normed * inner) / scale).astype(jnp.bfloat16)
    qg_terms = jnp.einsum("pthd,pthe->phde", query4, attn_grad, preferred_element_type=jnp.float32)
    first_qg = qg_terms[0]
    second_qg = qg_terms[1]
    higher_first = carried_in(first_qg, "seq", add_terms, zero_state, True)
    grad_second = carried_in(second_qg, "seq", add_terms, zero_state, False)
    total_second_qg = lax.psum(second_qg, "seq")
    grad_first = total_second_qg + higher_first
    later = jnp.stack([grad_first, grad_second]).astype(jnp.bfloat16)
    diffs = jnp.einsum("pthe,pshe->phts", attn_grad, value4, preferred_element_type=jnp.float32)
    diffs = jnp.where(mask, diffs, 0.0).astype(jnp.bfloat16)
    query_grad = jnp.einsum("phts,pshd->pthd", diffs, key4, preferred_element_type=jnp.float32)
    query_grad = query_grad + jnp.einsum(
        "pthe,phde->pthd", attn_grad, states, preferred_element_type=jnp.float32
    )
    key_grad = jnp.einsum("phts,pthd->pshd", diffs, query4, preferred_element_type=jnp.float32)
    key_grad = key_grad + jnp.einsum(
        "pshe,phde->pshd", value4, later, preferred_element_type=jnp.float32
    )
    value_grad = jnp.einsum(
        "phts,pthe->pshe", weights, attn_grad, preferred_element_type=jnp.float32
    )
    value_grad = value_grad + jnp.einsum(
        "pshd,phde->pshe", key4, later, preferred_element_type=jnp.float32
    )
    out_shape = (pair, length, width)
    return (
        output,
        query_grad.astype(jnp.bfloat16).reshape(out_shape),
        key_grad.astype(jnp.bfloat16).reshape(out_shape),
        value_grad.astype(jnp.bfloat16).reshape(out_shape),
        weight_grad,
    )


def on_device(*args):
    plan = on_eight_by_four if (lax.axis_size("seq"), lax.axis_size("head")) == (8, 4) else on_any_mesh
    return plan(*args)


def solution(mesh):
    rows = P(None, "seq", "head")
    return jax.shard_map(
        on_device,
        mesh=mesh,
        in_specs=(rows, rows, rows, P("head", None), rows),
        out_specs=(rows, rows, rows, rows, P("head", "seq")),
        check_vma=False,
    )
```

```python
import functools

import jax
import jax.numpy as jnp
from jax import lax
from jax.experimental import pallas as pl
from jax.experimental.pallas import tpu as pltpu
from jax.sharding import PartitionSpec as P

HEAD_DIM = 128
EPS = 1e-06
LASTING = {
    "kv": 3,
    "near": 3,
    "quarter": 0.2,
    "far": 0.01,
    "forward": 0.01,
    "join_kv": 0.01,
    "join_qg": 0.1,
    "project": 0.2,
    "inside": 5,
    "stack": 0.1,
    "last": 1,
}
WAITS = {
    "kv4.s": ["quarter", "a1.s", "near"],
    "h2.s": ["far", "a1.g"],
    "rs2.s": ["a2.s"],
    "a4.g": ["qg2.s", "qg1.g"],
    "g1.g": ["hy.g"],
    "qg4.g": ["h2.g", "rs2.g"],
    "h6.g": ["qg2.s"],
    "qg1.s": ["a2.g", "kv2.s"],
    "away": ["c2.g"],
    "qg4.s": ["rs2.s", "a4.s", "g1.s"],
    "hy.s": ["c3.g"],
    "forward": ["a1.g"],
    "qg2.s": ["a2.g"],
    "a2.s": ["c1.s"],
    "quarter": ["kv1.s"],
    "kv1.g": ["c1.s"],
    "g3.g": ["qg4.g"],
    "hz.g": ["qg4.g"],
    "c1.s": ["c2.s"],
    "c2.s": ["kv1.s"],
    "hz.s": ["rs2.s", "h4.g"],
    "qg2.g": ["g1.s"],
    "g1.s": ["h6.g"],
}

NN = (((1,), (0,)), ((), ()))
NT = (((1,), (1,)), ((), ()))
TN = (((0,), (0,)), ((), ()))


def mm(a, b, dims):
    return lax.dot_general(a, b, dims, preferred_element_type=jnp.float32)


def head_cols(i):
    return slice(i * HEAD_DIM, (i + 1) * HEAD_DIM)


def lower(length):
    rows = lax.broadcasted_iota(jnp.int32, (length, length), 0)
    cols = lax.broadcasted_iota(jnp.int32, (length, length), 1)
    return rows >= cols


def xor_permute(x, axis, bit):
    count = lax.axis_size(axis)
    return lax.ppermute(x, axis, [(i, i ^ bit) for i in range(count)])


def whole(n):
    return [pl.BlockSpec(memory_space=pltpu.VMEM)] * n


def lasting(name):
    return pl.CostEstimate(flops=int(LASTING[name] * 1.1e9), bytes_accessed=0, transcendentals=0)


def kernel_call(name, body, outs, args, vmem=16 * 2**20):
    return pl.pallas_call(
        body,
        out_shape=outs,
        in_specs=whole(len(args)),
        out_specs=whole(len(outs)),
        compiler_params=pltpu.CompilerParams(vmem_limit_bytes=vmem),
        cost_estimate=lasting(name),
        name=name,
    )(*args)


def shaped(shape, dtype):
    return jax.ShapeDtypeStruct(shape, dtype)


def kv_body(k_hbm, v_hbm, own_ref, send_ref, k_ref, v_ref, sems):
    loads = [
        pltpu.make_async_copy(k_hbm, k_ref, sems.at[0]),
        pltpu.make_async_copy(v_hbm, v_ref, sems.at[1]),
    ]
    for load in loads:
        load.start()
    for load in loads:
        load.wait()
    for i in range(k_ref.shape[2] // HEAD_DIM):
        c = head_cols(i)
        first = mm(k_ref[0, :, c], v_ref[0, :, c], TN)
        second = mm(k_ref[1, :, c], v_ref[1, :, c], TN)
        own_ref[i] = first
        send_ref[0, i] = first.astype(jnp.bfloat16)
        send_ref[1, i] = (first + second).astype(jnp.bfloat16)


def in_hbm(x):
    return pltpu.with_memory_space_constraint(x, pltpu.HBM)


def kv_products(keys, values):
    heads = keys.shape[2] // HEAD_DIM
    square = (heads, HEAD_DIM, HEAD_DIM)
    return pl.pallas_call(
        kv_body,
        out_shape=(shaped(square, jnp.float32), shaped((2,) + square, jnp.bfloat16)),
        in_specs=[pl.BlockSpec(memory_space=pltpu.HBM)] * 2,
        out_specs=whole(2),
        scratch_shapes=[
            pltpu.VMEM(keys.shape, keys.dtype),
            pltpu.VMEM(values.shape, values.dtype),
            pltpu.SemaphoreType.DMA((2,)),
        ],
        compiler_params=pltpu.CompilerParams(vmem_limit_bytes=16 * 2**20),
    )(keys, values)


def join_body(a_ref, b_ref, out_ref):
    out_ref[...] = (a_ref[...].astype(jnp.float32) + b_ref[...].astype(jnp.float32)).astype(out_ref.dtype)


def column_loads(spot_ref, w_hbm, w_ref, sems):
    n, _, cols = w_ref.shape
    loads = []
    for slot in range(n):
        at = pl.multiple_of((spot_ref[1] ^ slot) * cols, cols)
        loads.append(pltpu.make_async_copy(w_hbm.at[:, pl.ds(at, cols)], w_ref.at[slot], sems.at[slot]))
    return loads


def near_body(spot_ref, w_hbm, up_hbm, out_ref, up_ref, w_ref, sems):
    loads = [pltpu.make_async_copy(up_hbm, up_ref, sems.at[1])] + column_loads(spot_ref, w_hbm, w_ref, sems)
    for load in loads:
        load.start()
    for load in loads:
        load.wait()
    out_ref[...] = mm(up_ref[...], w_ref[0], NT)


def near_grad_of(up, weight, spot):
    rows, cols = up.shape
    features = weight.shape[0]
    return pl.pallas_call(
        near_body,
        out_shape=(shaped((rows, features), jnp.float32), shaped(up.shape, up.dtype)),
        in_specs=[pl.BlockSpec(memory_space=pltpu.SMEM)] + [pl.BlockSpec(memory_space=pltpu.HBM)] * 2,
        out_specs=whole(2),
        scratch_shapes=[pltpu.VMEM((1, features, cols), weight.dtype), pltpu.SemaphoreType.DMA((2,))],
        compiler_params=pltpu.CompilerParams(vmem_limit_bytes=16 * 2**20),
        cost_estimate=lasting("near"),
        name="near",
    )(spot, weight, up)


def far_body(n, spot_ref, w_hbm, before_ref, *refs):
    chunks, (out_ref, w_ref, sems) = refs[: n - 1], refs[n - 1 :]
    loads = column_loads(spot_ref, w_hbm, w_ref, sems)
    for load in loads[1:] + loads[:1]:
        load.start()
    total = before_ref[...]
    for slot in range(1, n):
        loads[slot].wait()
        total += mm(chunks[slot - 1][...], w_ref[slot], NT)
    out_ref[...] = total
    loads[0].wait()


def hidden_grad_of(before, chunks, weight, spot):
    rows, cols = chunks[0].shape
    features = weight.shape[0]
    n = len(chunks) + 1
    return pl.pallas_call(
        functools.partial(far_body, n),
        out_shape=(shaped((rows, features), jnp.float32), shaped((n, features, cols), weight.dtype)),
        in_specs=[pl.BlockSpec(memory_space=pltpu.SMEM), pl.BlockSpec(memory_space=pltpu.HBM)] + whole(n),
        out_specs=whole(2),
        scratch_shapes=[pltpu.SemaphoreType.DMA((n,))],
        compiler_params=pltpu.CompilerParams(vmem_limit_bytes=16 * 2**20),
        cost_estimate=lasting("far"),
        name="far",
    )(spot, weight, before, *chunks)


def forward_body(q_ref, k_ref, v_ref, hg_ref, own_ref, below_ref, above_ref,
                 state_ref, hidden_ref, g_ref, qown_ref, qsend_ref):
    length = q_ref.shape[1]
    mask = lower(length)
    heads = q_ref.shape[2] // HEAD_DIM
    blocks = [(i, p) for i in range(heads) for p in range(2)]
    rows = [slice(p * length, (p + 1) * length) for p in range(2)]
    queries = {(i, p): q_ref[p, :, head_cols(i)] for i, p in blocks}
    scores = {(i, p): mm(queries[i, p], k_ref[p, :, head_cols(i)], NT) for i, p in blocks}
    states = {}
    for i in range(heads):
        below = below_ref[i]
        states[i, 0] = below.astype(jnp.bfloat16)
        states[i, 1] = (below + own_ref[i] + above_ref[i]).astype(jnp.bfloat16)
    carried = {b: mm(queries[b], states[b], NN) for b in blocks}
    weights = {b: jnp.where(mask, scores[b], 0.0).astype(jnp.bfloat16) for b in blocks}
    attended = {(i, p): mm(weights[i, p], v_ref[p, :, head_cols(i)], NN) + carried[i, p] for i, p in blocks}
    squares = {b: jnp.mean(attended[b] * attended[b], axis=-1, keepdims=True) for b in blocks}
    inverse = {b: lax.rsqrt(squares[b] + EPS) for b in blocks}
    normed = {b: attended[b] * inverse[b] for b in blocks}
    grads = {(i, p): hg_ref[rows[p], head_cols(i)] for i, p in blocks}
    inner = {b: jnp.mean(grads[b] * normed[b], axis=-1, keepdims=True) for b in blocks}
    g = {b: ((grads[b] - normed[b] * inner[b]) * inverse[b]).astype(jnp.bfloat16) for b in blocks}
    terms = {b: mm(queries[b], g[b], TN) for b in blocks}
    for i, p in blocks:
        state_ref[p, i] = states[i, p]
        hidden_ref[rows[p], head_cols(i)] = normed[i, p].astype(jnp.bfloat16)
        g_ref[p, :, head_cols(i)] = g[i, p]
    for i in range(heads):
        qown_ref[i] = terms[i, 1]
        qsend_ref[0, i] = terms[i, 1].astype(jnp.bfloat16)
        qsend_ref[1, i] = (terms[i, 0] + terms[i, 1]).astype(jnp.bfloat16)


def inside_body(q_ref, k_ref, v_ref, g_ref, state_ref, dq_ref, dk_ref, dv_ref):
    length = q_ref.shape[1]
    mask = lower(length)
    for i in range(q_ref.shape[2] // HEAD_DIM):
        c = head_cols(i)
        for p in range(2):
            q, k, v, g = q_ref[p, :, c], k_ref[p, :, c], v_ref[p, :, c], g_ref[p, :, c]
            weights = jnp.where(mask, mm(q, k, NT), 0.0).astype(jnp.bfloat16)
            diffs = jnp.where(mask, mm(g, v, NT), 0.0).astype(jnp.bfloat16)
            dq_ref[p, :, c] = (mm(diffs, k, NN) + mm(g, state_ref[p, i], NT)).astype(jnp.bfloat16)
            dk_ref[p, :, c] = mm(diffs, q, TN)
            dv_ref[p, :, c] = mm(weights, g, TN)


def last_body(slots, spot_ref, k_ref, v_ref, dkp_ref, dvp_ref, own_ref, below_ref, above_ref, sum_ref, got_ref, *refs):
    hiddens, ups = refs[: len(slots)], refs[len(slots)]
    outs, sems = refs[len(slots) + 1 : len(slots) + 5], refs[-1]
    dk_ref, dv_ref, out_ref, weight_ref = refs[len(slots) + 5 : -1]
    features = weight_ref.shape[0]
    tile = features // 2
    copies = [pltpu.make_async_copy(x, y, sems.at[i]) for i, (x, y) in enumerate(zip((dk_ref, dv_ref, out_ref), outs))]
    copies += [
        pltpu.make_async_copy(weight_ref.at[pl.ds(t * tile, tile)], outs[3].at[pl.ds(t * tile, tile)], sems.at[3 + t])
        for t in range(2)
    ]
    out_ref[...] = (sum_ref[...] + got_ref[...].astype(jnp.float32)).astype(out_ref.dtype)
    copies[2].start()
    for i in range(k_ref.shape[2] // HEAD_DIM):
        c = head_cols(i)
        below = below_ref[i]
        laters = (below + own_ref[i] + above_ref[i], below)
        for p in range(2):
            later = laters[p].astype(jnp.bfloat16)
            k, v = k_ref[p, :, c], v_ref[p, :, c]
            dk_ref[p, :, c] = (dkp_ref[p, :, c] + mm(v, later, NT)).astype(jnp.bfloat16)
            dv_ref[p, :, c] = (dvp_ref[p, :, c] + mm(k, later, NN)).astype(jnp.bfloat16)
    copies[0].start()
    copies[1].start()
    head = spot_ref[1]
    n, _, share, _ = ups.shape
    rights = jnp.concatenate([ups[m, slot] for group in slots for slot in group for m in range(n)])
    for t in range(2):
        lefts = [
            ref[i, pl.ds(pl.multiple_of((head ^ m) * share, share), share), t * tile : (t + 1) * tile]
            for ref, group in zip(hiddens, slots)
            for i in range(len(group))
            for m in range(n)
        ]
        weight_ref[t * tile : (t + 1) * tile, :] = mm(jnp.concatenate(lefts), rights, TN)
        copies[3 + t].start()
    for copy in copies:
        copy.wait()


def last_call(slots, shapes, spot, args):
    n = len(args)
    return pl.pallas_call(
        functools.partial(last_body, slots),
        out_shape=shapes,
        in_specs=[pl.BlockSpec(memory_space=pltpu.SMEM)] + whole(n),
        out_specs=[pl.BlockSpec(memory_space=pl.ANY)] * len(shapes),
        scratch_shapes=[pltpu.VMEM(x.shape, x.dtype) for x in shapes] + [pltpu.SemaphoreType.DMA((5,))],
        compiler_params=pltpu.CompilerParams(vmem_limit_bytes=24 * 2**20),
        cost_estimate=lasting("last"),
        name="last",
    )(spot, *args)


def project_body(slots, w_ref, hidden_ref, out_ref):
    for i, slot in enumerate(slots):
        out_ref[i] = mm(hidden_ref[...], w_ref[slot], NN).astype(out_ref.dtype)


def project(hidden, by_columns, slots, dtype):
    shape = (len(slots), hidden.shape[0], by_columns.shape[2])
    return kernel_call("project", functools.partial(project_body, slots), (shaped(shape, dtype),), (by_columns, hidden))[0]


def quarter_body(n, spot_ref, *refs):
    chunks, keep_ref, send_ref = refs[:n], refs[-2], refs[-1]
    seq, head = spot_ref[0], spot_ref[1]
    share, cols = keep_ref.shape[1:]
    rows = pl.ds(pl.multiple_of(head * share, share), share)
    odd = seq & 1
    for m in range(n):
        t = (seq // 2) ^ head ^ m
        entry = (t & 1) * (n // 2) + t // 2
        keep_ref[entry] = chunks[m][rows, pl.ds(pl.multiple_of(odd * cols, cols), cols)]
        send_ref[entry] = chunks[m][rows, pl.ds(pl.multiple_of((1 - odd) * cols, cols), cols)]


def share_out(chunks, spot):
    n = len(chunks)
    rows, cols = chunks[0].shape
    part = shaped((n, rows // n, cols // 2), chunks[0].dtype)
    return pl.pallas_call(
        functools.partial(quarter_body, n),
        out_shape=(part, part),
        in_specs=[pl.BlockSpec(memory_space=pltpu.SMEM)] + whole(n),
        out_specs=whole(2),
        compiler_params=pltpu.CompilerParams(vmem_limit_bytes=16 * 2**20),
        cost_estimate=lasting("quarter"),
        name="quarter",
    )(spot, *chunks)


def stack_body(*refs):
    for i, ref in enumerate(refs[:-1]):
        refs[-1][i] = ref[...]


def stacked(blocks):
    shape = (len(blocks),) + blocks[0].shape
    return kernel_call("stack", stack_body, (shaped(shape, blocks[0].dtype),), blocks)[0]


def after(x, *others):
    if not others:
        return x
    return lax.optimization_barrier((x,) + others)[0]


def on_eight_by_four(queries, keys, values, out_weight, upstream):
    pair, length, width = queries.shape
    heads = width // HEAD_DIM
    n_seq, n_head = lax.axis_size("seq"), lax.axis_size("head")
    seq, head = lax.axis_index("seq"), lax.axis_index("head")
    rows, own_cols = pair * length, upstream.shape[2]
    f32, bf16 = jnp.float32, jnp.bfloat16
    square = (heads, HEAD_DIM, HEAD_DIM)
    flat_up = upstream.reshape(rows, own_cols)
    spot = jnp.stack([seq, head]).astype(jnp.int32)
    seen = {}

    def node(name, x):
        early = [seen[other] for other in WAITS.get(name, ()) if other in seen]
        if early:
            x = after(x, *early)
        seen[name] = x
        return x

    class Scan:
        def __init__(self, tag, near, send):
            self.tag, self.send = tag, send
            self.below = jnp.zeros_like(near)
            self.above = jnp.zeros_like(near)

        def put(self, bit):
            self.upper = (seq & bit) != 0
            if 2 * bit == n_seq:
                self.send = jnp.where(self.upper, self.send[1], self.send[0])
            self.name = self.tag + str(bit)
            self.send = node(self.name + ".s", self.send)
            self.raw = xor_permute(self.send, "seq", bit)

        def take(self):
            got = node(self.name + ".g", self.raw)
            if got.ndim == 4:
                self.send = kernel_call("join_" + self.tag, join_body, (shaped(got.shape, got.dtype),), (self.send, got))[0]
            self.add(got.astype(jnp.float32))

        def add(self, got):
            near, both = (got[0], got[1]) if got.ndim == 4 else (got, got)
            self.below = jnp.where(self.upper, self.below + near, self.below)
            self.above = jnp.where(self.upper, self.above, self.above + both)

    kv_own, kv_send = kv_products(in_hbm(keys), in_hbm(values))
    kv = Scan("kv", kv_own, kv_send)
    kv.put(1)
    seen["kv"] = kv_send
    flat_up = after(flat_up, kv_send)
    c2_raw = xor_permute(node("c2.s", flat_up), "head", 2)
    c1_raw = xor_permute(node("c1.s", flat_up), "head", 1)
    weight_hbm = in_hbm(out_weight)
    near_grad, c0 = near_grad_of(in_hbm(node("near", flat_up)), weight_hbm, spot)
    near_grad = node("near_out", near_grad)
    kv.take()
    kv.put(2)
    c2 = node("c2.g", c2_raw)
    c3_raw = xor_permute(node("c3.s", c2), "head", 1)
    c1 = node("c1.g", c1_raw)
    c3 = node("c3.g", c3_raw)
    chunks = [c0, c1, c2, c3]
    keep, a1_send = share_out([node("quarter", c0)] + chunks[1:], spot)
    a1_raw = xor_permute(node("a1.s", a1_send), "seq", 1)
    kv.take()
    kv.put(4)
    a1 = node("a1.g", a1_raw)
    held = jnp.stack([keep, a1], axis=1)
    a2_raw = xor_permute(node("a2.s", held[2:]), "seq", 2)
    hidden_grad, by_columns = hidden_grad_of(node("far", near_grad), chunks[1:], weight_hbm, spot)
    a2 = node("a2.g", a2_raw)
    held = jnp.concatenate([held[:2], a2], axis=1)
    a4_raw = xor_permute(node("a4.s", held[1]), "seq", 4)
    kv.take()
    states, hidden, attn_grad, qg_own, qg_send = kernel_call(
        "forward",
        forward_body,
        (
            shaped((2,) + square, bf16),
            shaped((rows, width), bf16),
            shaped((pair, length, width), bf16),
            shaped(square, f32),
            shaped((2,) + square, bf16),
        ),
        (queries, keys, values, node("forward", hidden_grad), kv_own, kv.below, kv.above),
    )
    qg = Scan("qg", qg_own, qg_send)
    qg.put(1)
    h2_raw = xor_permute(node("h2.s", hidden), "seq", 2)
    h4_raw = xor_permute(node("h4.s", hidden), "seq", 4)
    away = project(node("away", hidden), by_columns, range(1, n_head, 2), bf16)
    rs1_raw = xor_permute(node("rs1.s", away), "head", 1)
    home = project(node("home", hidden), by_columns, range(0, n_head, 2), f32)
    qg.take()
    qg.put(2)
    h2 = node("h2.g", h2_raw)
    first_rows = stacked([hidden, h2])
    hy_raw = xor_permute(node("hy.s", first_rows), "seq", 1)
    rs1 = node("rs1.g", rs1_raw)
    total = (home + rs1.astype(f32)).reshape(2, rows, own_cols)
    rs2_raw = xor_permute(node("rs2.s", total[1].astype(bf16)), "head", 2)

    query_grad, key_part, value_part = kernel_call(
        "inside",
        inside_body,
        (
            shaped((pair, length, width), bf16),
            shaped((pair, length, width), f32),
            shaped((pair, length, width), f32),
        ),
        (queries, keys, values, node("inside", attn_grad), states),
    )
    ups = jnp.concatenate([held[0], node("a4.g", a4_raw)])
    h4 = node("h4.g", h4_raw)
    g2_raw = xor_permute(node("g2.s", ups), "head", 2)
    h6_raw = xor_permute(node("h6.s", h4), "seq", 2)
    h6 = node("h6.g", h6_raw)
    second_rows = stacked([h4, h6])
    hz_raw = xor_permute(node("hz.s", second_rows), "seq", 1)
    g1_raw = xor_permute(node("g1.s", ups), "head", 1)
    qg.take()
    qg.put(4)
    g2 = node("g2.g", g2_raw)
    g3_raw = xor_permute(node("g3.s", g2), "head", 1)
    hy = node("hy.g", hy_raw)
    g1 = node("g1.g", g1_raw)
    rs2 = node("rs2.g", rs2_raw)
    qg.take()
    hz = node("hz.g", hz_raw)
    g3 = node("g3.g", g3_raw)
    ups = jnp.stack([ups, g1, g2, g3])
    key_grad, value_grad, output, weight_grad = last_call(
        [[0, 2], [1, 3], [4, 6], [5, 7]],
        (
            shaped((pair, length, width), bf16),
            shaped((pair, length, width), bf16),
            shaped((rows, own_cols), bf16),
            shaped((width, own_cols // 2), f32),
        ),
        spot,
        [keys, values, node("final", key_part), value_part, qg_own, qg.below, qg.above, total[0], rs2]
        + [first_rows, hy, second_rows, hz, ups],
    )
    return (
        output.reshape(pair, length, -1),
        query_grad,
        key_grad,
        value_grad,
        weight_grad,
    )


def carried_in(shard, axis, join, neutral, backward):
    count = lax.axis_size(axis)
    place = lax.axis_index(axis)
    ahead = count - 1 - place if backward else place
    gathered = lax.all_gather(shard.astype(jnp.bfloat16), axis)
    state = jnp.zeros_like(shard) + jnp.asarray(neutral, shard.dtype)

    def one(lap, state):
        source = count - 1 - lap if backward else lap
        return join(state, lax.dynamic_index_in_dim(gathered, source, 0, False).astype(shard.dtype))

    return lax.fori_loop(0, ahead, one, state)


def add_terms(earlier, later):
    return jax.tree.map(lambda left, right: left + right, earlier, later)


def on_any_mesh(queries, keys, values, out_weight, upstream):
    pair, length, width = queries.shape
    heads_here = width // HEAD_DIM
    shape_four = (pair, length, heads_here, HEAD_DIM)
    query4 = queries.reshape(shape_four)
    key4 = keys.reshape(shape_four)
    value4 = values.reshape(shape_four)
    kv_terms = jnp.einsum("pchd,pche->phde", key4, value4, preferred_element_type=jnp.float32)
    first_kv = kv_terms[0]
    second_kv = kv_terms[1]
    zero_state = jnp.zeros_like(first_kv)
    before = carried_in(first_kv, "seq", add_terms, zero_state, False)
    after = carried_in(second_kv, "seq", add_terms, zero_state, True)
    total_first = lax.psum(first_kv, "seq")
    state_second = total_first + after
    states = jnp.stack([before, state_second]).astype(jnp.bfloat16)
    mask = lower(length)
    scores = jnp.einsum("pthd,pshd->phts", query4, key4, preferred_element_type=jnp.float32)
    weights = jnp.where(mask, scores, 0.0).astype(jnp.bfloat16)
    attended = jnp.einsum("phts,pshe->pthe", weights, value4, preferred_element_type=jnp.float32)
    attended = attended + jnp.einsum(
        "pthd,phde->pthe", query4, states, preferred_element_type=jnp.float32
    )
    scale = jnp.sqrt(jnp.mean(attended * attended, axis=-1, keepdims=True) + EPS)
    normed = attended / scale
    hidden = normed.astype(jnp.bfloat16).reshape(pair * length, width)
    partial_out = jnp.dot(hidden, out_weight, preferred_element_type=jnp.float32)
    output = lax.psum_scatter(
        partial_out.astype(jnp.bfloat16), "head", scatter_dimension=1, tiled=True
    ).astype(jnp.float32)
    output = output.astype(jnp.bfloat16).reshape(pair, length, -1)
    flat_up = upstream.reshape(pair * length, upstream.shape[2])
    full_up = lax.all_gather(flat_up, "head", axis=1, tiled=True)
    hidden_grad = lax.dot_general(
        full_up, out_weight, (((1,), (1,)), ((), ())), preferred_element_type=jnp.float32
    )
    weight_share = lax.psum_scatter(
        lax.dot_general(
            full_up, hidden, (((0,), (0,)), ((), ())), preferred_element_type=jnp.float32
        ),
        "seq",
        scatter_dimension=0,
        tiled=True,
    )
    weight_grad = weight_share.T
    grad_four = hidden_grad.reshape(shape_four)
    inner = jnp.mean(grad_four * normed, axis=-1, keepdims=True)
    attn_grad = ((grad_four - normed * inner) / scale).astype(jnp.bfloat16)
    qg_terms = jnp.einsum("pthd,pthe->phde", query4, attn_grad, preferred_element_type=jnp.float32)
    first_qg = qg_terms[0]
    second_qg = qg_terms[1]
    higher_first = carried_in(first_qg, "seq", add_terms, zero_state, True)
    grad_second = carried_in(second_qg, "seq", add_terms, zero_state, False)
    total_second_qg = lax.psum(second_qg, "seq")
    grad_first = total_second_qg + higher_first
    later = jnp.stack([grad_first, grad_second]).astype(jnp.bfloat16)
    diffs = jnp.einsum("pthe,pshe->phts", attn_grad, value4, preferred_element_type=jnp.float32)
    diffs = jnp.where(mask, diffs, 0.0).astype(jnp.bfloat16)
    query_grad = jnp.einsum("phts,pshd->pthd", diffs, key4, preferred_element_type=jnp.float32)
    query_grad = query_grad + jnp.einsum(
        "pthe,phde->pthd", attn_grad, states, preferred_element_type=jnp.float32
    )
    key_grad = jnp.einsum("phts,pthd->pshd", diffs, query4, preferred_element_type=jnp.float32)
    key_grad = key_grad + jnp.einsum(
        "pshe,phde->pshd", value4, later, preferred_element_type=jnp.float32
    )
    value_grad = jnp.einsum(
        "phts,pthe->pshe", weights, attn_grad, preferred_element_type=jnp.float32
    )
    value_grad = value_grad + jnp.einsum(
        "pshd,phde->pshe", key4, later, preferred_element_type=jnp.float32
    )
    out_shape = (pair, length, width)
    return (
        output,
        query_grad.astype(jnp.bfloat16).reshape(out_shape),
        key_grad.astype(jnp.bfloat16).reshape(out_shape),
        value_grad.astype(jnp.bfloat16).reshape(out_shape),
        weight_grad,
    )


def on_device(*args):
    plan = on_eight_by_four if (lax.axis_size("seq"), lax.axis_size("head")) == (8, 4) else on_any_mesh
    return plan(*args)


def solution(mesh):
    rows = P(None, "seq", "head")
    return jax.shard_map(
        on_device,
        mesh=mesh,
        in_specs=(rows, rows, rows, P("head", None), rows),
        out_specs=(rows, rows, rows, rows, P("head", "seq")),
        check_vma=False,
    )
```

```python
import functools

import jax
import jax.numpy as jnp
from jax import lax
from jax.experimental import pallas as pl
from jax.experimental.pallas import tpu as pltpu
from jax.sharding import PartitionSpec as P

HEAD_DIM = 128
EPS = 1e-06
LASTING = {
    "kv": 3,
    "near": 3,
    "quarter": 0.2,
    "far": 0.01,
    "forward": 0.01,
    "join_kv": 0.01,
    "join_qg": 0.1,
    "project": 0.2,
    "inside": 5,
    "stack": 0.1,
    "last": 1,
}
WAITS = {
    "kv4.s": ["quarter", "a1.s", "near"],
    "h2.s": ["far", "a1.g"],
    "rs2.s": ["a2.s"],
    "a4.g": ["qg2.s", "qg1.g"],
    "g1.g": ["hy.g"],
    "qg4.g": ["h2.g", "rs2.g"],
    "h6.g": ["qg2.s"],
    "qg1.s": ["a2.g", "kv2.s"],
    "away": ["c2.g"],
    "qg4.s": ["rs2.s", "a4.s", "g1.s"],
    "hy.s": ["c3.g"],
    "forward": ["a1.g"],
    "qg2.s": ["a2.g"],
    "a2.s": ["c1.s"],
    "quarter": ["kv1.s"],
    "kv1.g": ["c1.s"],
    "g3.g": ["qg4.g"],
    "hz.g": ["qg4.g"],
    "c1.s": ["c2.s"],
    "c2.s": ["kv1.s"],
    "hz.s": ["rs2.s", "h4.g"],
    "qg2.g": ["g1.s"],
    "g1.s": ["h6.g"],
}

NN = (((1,), (0,)), ((), ()))
NT = (((1,), (1,)), ((), ()))
TN = (((0,), (0,)), ((), ()))


def mm(a, b, dims):
    return lax.dot_general(a, b, dims, preferred_element_type=jnp.float32)


def head_cols(i):
    return slice(i * HEAD_DIM, (i + 1) * HEAD_DIM)


def lower(length):
    rows = lax.broadcasted_iota(jnp.int32, (length, length), 0)
    cols = lax.broadcasted_iota(jnp.int32, (length, length), 1)
    return rows >= cols


def xor_permute(x, axis, bit):
    count = lax.axis_size(axis)
    return lax.ppermute(x, axis, [(i, i ^ bit) for i in range(count)])


def whole(n):
    return [pl.BlockSpec(memory_space=pltpu.VMEM)] * n


def lasting(name):
    return pl.CostEstimate(flops=int(LASTING[name] * 1.1e9), bytes_accessed=0, transcendentals=0)


def kernel_call(name, body, outs, args, vmem=16 * 2**20):
    return pl.pallas_call(
        body,
        out_shape=outs,
        in_specs=whole(len(args)),
        out_specs=whole(len(outs)),
        compiler_params=pltpu.CompilerParams(vmem_limit_bytes=vmem),
        cost_estimate=lasting(name),
        name=name,
    )(*args)


def shaped(shape, dtype):
    return jax.ShapeDtypeStruct(shape, dtype)


def kv_body(k_hbm, v_hbm, own_ref, send_ref, k_ref, v_ref, sems):
    loads = [
        pltpu.make_async_copy(k_hbm, k_ref, sems.at[0]),
        pltpu.make_async_copy(v_hbm, v_ref, sems.at[1]),
    ]
    for load in loads:
        load.start()
    for load in loads:
        load.wait()
    heads = k_ref.shape[2] // HEAD_DIM
    products = [[mm(k_ref[p, :, head_cols(i)], v_ref[p, :, head_cols(i)], TN) for p in range(2)] for i in range(heads)]
    for i, (first, second) in enumerate(products):
        own_ref[i] = first
        send_ref[0, i] = first.astype(jnp.bfloat16)
        send_ref[1, i] = (first + second).astype(jnp.bfloat16)


def in_hbm(x):
    return pltpu.with_memory_space_constraint(x, pltpu.HBM)


def kv_products(keys, values):
    heads = keys.shape[2] // HEAD_DIM
    square = (heads, HEAD_DIM, HEAD_DIM)
    return pl.pallas_call(
        kv_body,
        out_shape=(shaped(square, jnp.float32), shaped((2,) + square, jnp.bfloat16)),
        in_specs=[pl.BlockSpec(memory_space=pltpu.HBM)] * 2,
        out_specs=whole(2),
        scratch_shapes=[
            pltpu.VMEM(keys.shape, keys.dtype),
            pltpu.VMEM(values.shape, values.dtype),
            pltpu.SemaphoreType.DMA((2,)),
        ],
        compiler_params=pltpu.CompilerParams(vmem_limit_bytes=16 * 2**20),
    )(keys, values)


def join_body(a_ref, b_ref, out_ref):
    out_ref[...] = (a_ref[...].astype(jnp.float32) + b_ref[...].astype(jnp.float32)).astype(out_ref.dtype)


def column_loads(spot_ref, w_hbm, w_ref, sems):
    n, _, cols = w_ref.shape
    loads = []
    for slot in range(n):
        at = pl.multiple_of((spot_ref[1] ^ slot) * cols, cols)
        loads.append(pltpu.make_async_copy(w_hbm.at[:, pl.ds(at, cols)], w_ref.at[slot], sems.at[slot]))
    return loads


def near_body(spot_ref, w_hbm, up_hbm, out_ref, up_ref, w_ref, sems):
    loads = [pltpu.make_async_copy(up_hbm, up_ref, sems.at[1])] + column_loads(spot_ref, w_hbm, w_ref, sems)
    for load in loads:
        load.start()
    for load in loads:
        load.wait()
    out_ref[...] = mm(up_ref[...], w_ref[0], NT)


def near_grad_of(up, weight, spot):
    rows, cols = up.shape
    features = weight.shape[0]
    return pl.pallas_call(
        near_body,
        out_shape=(shaped((rows, features), jnp.float32), shaped(up.shape, up.dtype)),
        in_specs=[pl.BlockSpec(memory_space=pltpu.SMEM)] + [pl.BlockSpec(memory_space=pltpu.HBM)] * 2,
        out_specs=whole(2),
        scratch_shapes=[pltpu.VMEM((1, features, cols), weight.dtype), pltpu.SemaphoreType.DMA((2,))],
        compiler_params=pltpu.CompilerParams(vmem_limit_bytes=16 * 2**20),
        cost_estimate=lasting("near"),
        name="near",
    )(spot, weight, up)


def far_body(n, spot_ref, w_hbm, before_ref, *refs):
    chunks, (out_ref, w_ref, sems) = refs[: n - 1], refs[n - 1 :]
    loads = column_loads(spot_ref, w_hbm, w_ref, sems)
    for load in loads[1:] + loads[:1]:
        load.start()
    total = before_ref[...]
    for slot in range(1, n):
        loads[slot].wait()
        total += mm(chunks[slot - 1][...], w_ref[slot], NT)
    out_ref[...] = total
    loads[0].wait()


def hidden_grad_of(before, chunks, weight, spot):
    rows, cols = chunks[0].shape
    features = weight.shape[0]
    n = len(chunks) + 1
    return pl.pallas_call(
        functools.partial(far_body, n),
        out_shape=(shaped((rows, features), jnp.float32), shaped((n, features, cols), weight.dtype)),
        in_specs=[pl.BlockSpec(memory_space=pltpu.SMEM), pl.BlockSpec(memory_space=pltpu.HBM)] + whole(n),
        out_specs=whole(2),
        scratch_shapes=[pltpu.SemaphoreType.DMA((n,))],
        compiler_params=pltpu.CompilerParams(vmem_limit_bytes=16 * 2**20),
        cost_estimate=lasting("far"),
        name="far",
    )(spot, weight, before, *chunks)


def forward_body(q_ref, k_ref, v_ref, hg_ref, own_ref, below_ref, above_ref,
                 state_ref, hidden_ref, g_ref, qown_ref, qsend_ref):
    length = q_ref.shape[1]
    mask = lower(length)
    heads = q_ref.shape[2] // HEAD_DIM
    blocks = [(i, p) for i in range(heads) for p in range(2)]
    rows = [slice(p * length, (p + 1) * length) for p in range(2)]
    queries = {(i, p): q_ref[p, :, head_cols(i)] for i, p in blocks}
    scores = {(i, p): mm(queries[i, p], k_ref[p, :, head_cols(i)], NT) for i, p in blocks}
    states = {}
    for i in range(heads):
        below = below_ref[i]
        states[i, 0] = below.astype(jnp.bfloat16)
        states[i, 1] = (below + own_ref[i] + above_ref[i]).astype(jnp.bfloat16)
    carried = {b: mm(queries[b], states[b], NN) for b in blocks}
    weights = {b: jnp.where(mask, scores[b], 0.0).astype(jnp.bfloat16) for b in blocks}
    attended = {(i, p): mm(weights[i, p], v_ref[p, :, head_cols(i)], NN) + carried[i, p] for i, p in blocks}
    squares = {b: jnp.mean(attended[b] * attended[b], axis=-1, keepdims=True) for b in blocks}
    inverse = {b: lax.rsqrt(squares[b] + EPS) for b in blocks}
    normed = {b: attended[b] * inverse[b] for b in blocks}
    grads = {(i, p): hg_ref[rows[p], head_cols(i)] for i, p in blocks}
    inner = {b: jnp.mean(grads[b] * normed[b], axis=-1, keepdims=True) for b in blocks}
    g = {b: ((grads[b] - normed[b] * inner[b]) * inverse[b]).astype(jnp.bfloat16) for b in blocks}
    terms = {b: mm(queries[b], g[b], TN) for b in blocks}
    for i, p in blocks:
        state_ref[p, i] = states[i, p]
        hidden_ref[rows[p], head_cols(i)] = normed[i, p].astype(jnp.bfloat16)
        g_ref[p, :, head_cols(i)] = g[i, p]
    for i in range(heads):
        qown_ref[i] = terms[i, 1]
        qsend_ref[0, i] = terms[i, 1].astype(jnp.bfloat16)
        qsend_ref[1, i] = (terms[i, 0] + terms[i, 1]).astype(jnp.bfloat16)


def inside_body(q_ref, k_ref, v_ref, g_ref, state_ref, dq_ref, dk_ref, dv_ref):
    length = q_ref.shape[1]
    mask = lower(length)
    for i in range(q_ref.shape[2] // HEAD_DIM):
        c = head_cols(i)
        for p in range(2):
            q, k, v, g = q_ref[p, :, c], k_ref[p, :, c], v_ref[p, :, c], g_ref[p, :, c]
            weights = jnp.where(mask, mm(q, k, NT), 0.0).astype(jnp.bfloat16)
            diffs = jnp.where(mask, mm(g, v, NT), 0.0).astype(jnp.bfloat16)
            dq_ref[p, :, c] = (mm(diffs, k, NN) + mm(g, state_ref[p, i], NT)).astype(jnp.bfloat16)
            dk_ref[p, :, c] = mm(diffs, q, TN)
            dv_ref[p, :, c] = mm(weights, g, TN)


def last_body(slots, spot_ref, k_ref, v_ref, dkp_ref, dvp_ref, own_ref, below_ref, above_ref, sum_ref, got_ref, *refs):
    hiddens, ups = refs[: len(slots)], refs[len(slots)]
    outs, sems = refs[len(slots) + 1 : len(slots) + 5], refs[-1]
    dk_ref, dv_ref, out_ref, weight_ref = refs[len(slots) + 5 : -1]
    features = weight_ref.shape[0]
    tile = features // 2
    copies = [pltpu.make_async_copy(x, y, sems.at[i]) for i, (x, y) in enumerate(zip((dk_ref, dv_ref, out_ref), outs))]
    copies += [
        pltpu.make_async_copy(weight_ref.at[pl.ds(t * tile, tile)], outs[3].at[pl.ds(t * tile, tile)], sems.at[3 + t])
        for t in range(2)
    ]
    out_ref[...] = (sum_ref[...] + got_ref[...].astype(jnp.float32)).astype(out_ref.dtype)
    copies[2].start()
    blocks = [(i, p) for i in range(k_ref.shape[2] // HEAD_DIM) for p in range(2)]
    laters = {}
    for i, _ in blocks:
        below = below_ref[i]
        laters[i, 0] = (below + own_ref[i] + above_ref[i]).astype(jnp.bfloat16)
        laters[i, 1] = below.astype(jnp.bfloat16)
    dk = {(i, p): mm(v_ref[p, :, head_cols(i)], laters[i, p], NT) for i, p in blocks}
    dv = {(i, p): mm(k_ref[p, :, head_cols(i)], laters[i, p], NN) for i, p in blocks}
    for i, p in blocks:
        c = head_cols(i)
        dk_ref[p, :, c] = (dkp_ref[p, :, c] + dk[i, p]).astype(jnp.bfloat16)
        dv_ref[p, :, c] = (dvp_ref[p, :, c] + dv[i, p]).astype(jnp.bfloat16)
    copies[0].start()
    copies[1].start()
    head = spot_ref[1]
    n, _, share, _ = ups.shape
    rights = jnp.concatenate([ups[m, slot] for group in slots for slot in group for m in range(n)])
    for t in range(2):
        lefts = [
            ref[i, pl.ds(pl.multiple_of((head ^ m) * share, share), share), t * tile : (t + 1) * tile]
            for ref, group in zip(hiddens, slots)
            for i in range(len(group))
            for m in range(n)
        ]
        weight_ref[t * tile : (t + 1) * tile, :] = mm(jnp.concatenate(lefts), rights, TN)
        copies[3 + t].start()
    for copy in copies:
        copy.wait()


def last_call(slots, shapes, spot, args):
    n = len(args)
    return pl.pallas_call(
        functools.partial(last_body, slots),
        out_shape=shapes,
        in_specs=[pl.BlockSpec(memory_space=pltpu.SMEM)] + whole(n),
        out_specs=[pl.BlockSpec(memory_space=pl.ANY)] * len(shapes),
        scratch_shapes=[pltpu.VMEM(x.shape, x.dtype) for x in shapes] + [pltpu.SemaphoreType.DMA((5,))],
        compiler_params=pltpu.CompilerParams(vmem_limit_bytes=24 * 2**20),
        cost_estimate=lasting("last"),
        name="last",
    )(spot, *args)


def project_body(slots, w_ref, hidden_ref, out_ref):
    for i, slot in enumerate(slots):
        out_ref[i] = mm(hidden_ref[...], w_ref[slot], NN).astype(out_ref.dtype)


def project(hidden, by_columns, slots, dtype):
    shape = (len(slots), hidden.shape[0], by_columns.shape[2])
    return kernel_call("project", functools.partial(project_body, slots), (shaped(shape, dtype),), (by_columns, hidden))[0]


def quarter_body(n, spot_ref, *refs):
    chunks, keep_ref, send_ref = refs[:n], refs[-2], refs[-1]
    seq, head = spot_ref[0], spot_ref[1]
    share, cols = keep_ref.shape[1:]
    rows = pl.ds(pl.multiple_of(head * share, share), share)
    odd = seq & 1
    for m in range(n):
        t = (seq // 2) ^ head ^ m
        entry = (t & 1) * (n // 2) + t // 2
        keep_ref[entry] = chunks[m][rows, pl.ds(pl.multiple_of(odd * cols, cols), cols)]
        send_ref[entry] = chunks[m][rows, pl.ds(pl.multiple_of((1 - odd) * cols, cols), cols)]


def share_out(chunks, spot):
    n = len(chunks)
    rows, cols = chunks[0].shape
    part = shaped((n, rows // n, cols // 2), chunks[0].dtype)
    return pl.pallas_call(
        functools.partial(quarter_body, n),
        out_shape=(part, part),
        in_specs=[pl.BlockSpec(memory_space=pltpu.SMEM)] + whole(n),
        out_specs=whole(2),
        compiler_params=pltpu.CompilerParams(vmem_limit_bytes=16 * 2**20),
        cost_estimate=lasting("quarter"),
        name="quarter",
    )(spot, *chunks)


def stack_body(*refs):
    for i, ref in enumerate(refs[:-1]):
        refs[-1][i] = ref[...]


def stacked(blocks):
    shape = (len(blocks),) + blocks[0].shape
    return kernel_call("stack", stack_body, (shaped(shape, blocks[0].dtype),), blocks)[0]


def after(x, *others):
    if not others:
        return x
    return lax.optimization_barrier((x,) + others)[0]


def on_eight_by_four(queries, keys, values, out_weight, upstream):
    pair, length, width = queries.shape
    heads = width // HEAD_DIM
    n_seq, n_head = lax.axis_size("seq"), lax.axis_size("head")
    seq, head = lax.axis_index("seq"), lax.axis_index("head")
    rows, own_cols = pair * length, upstream.shape[2]
    f32, bf16 = jnp.float32, jnp.bfloat16
    square = (heads, HEAD_DIM, HEAD_DIM)
    flat_up = upstream.reshape(rows, own_cols)
    spot = jnp.stack([seq, head]).astype(jnp.int32)
    seen = {}

    def node(name, x):
        early = [seen[other] for other in WAITS.get(name, ()) if other in seen]
        if early:
            x = after(x, *early)
        seen[name] = x
        return x

    class Scan:
        def __init__(self, tag, near, send):
            self.tag, self.send = tag, send
            self.below = jnp.zeros_like(near)
            self.above = jnp.zeros_like(near)

        def put(self, bit):
            self.upper = (seq & bit) != 0
            if 2 * bit == n_seq:
                self.send = jnp.where(self.upper, self.send[1], self.send[0])
            self.name = self.tag + str(bit)
            self.send = node(self.name + ".s", self.send)
            self.raw = xor_permute(self.send, "seq", bit)

        def take(self):
            got = node(self.name + ".g", self.raw)
            if got.ndim == 4:
                self.send = kernel_call("join_" + self.tag, join_body, (shaped(got.shape, got.dtype),), (self.send, got))[0]
            self.add(got.astype(jnp.float32))

        def add(self, got):
            near, both = (got[0], got[1]) if got.ndim == 4 else (got, got)
            self.below = jnp.where(self.upper, self.below + near, self.below)
            self.above = jnp.where(self.upper, self.above, self.above + both)

    kv_own, kv_send = kv_products(in_hbm(keys), in_hbm(values))
    kv = Scan("kv", kv_own, kv_send)
    kv.put(1)
    seen["kv"] = kv_send
    flat_up = after(flat_up, kv_send)
    c2_raw = xor_permute(node("c2.s", flat_up), "head", 2)
    c1_raw = xor_permute(node("c1.s", flat_up), "head", 1)
    weight_hbm = in_hbm(out_weight)
    near_grad, c0 = near_grad_of(in_hbm(node("near", flat_up)), weight_hbm, spot)
    near_grad = node("near_out", near_grad)
    kv.take()
    kv.put(2)
    c2 = node("c2.g", c2_raw)
    c3_raw = xor_permute(node("c3.s", c2), "head", 1)
    c1 = node("c1.g", c1_raw)
    c3 = node("c3.g", c3_raw)
    chunks = [c0, c1, c2, c3]
    keep, a1_send = share_out([node("quarter", c0)] + chunks[1:], spot)
    a1_raw = xor_permute(node("a1.s", a1_send), "seq", 1)
    kv.take()
    kv.put(4)
    a1 = node("a1.g", a1_raw)
    held = jnp.stack([keep, a1], axis=1)
    a2_raw = xor_permute(node("a2.s", held[2:]), "seq", 2)
    hidden_grad, by_columns = hidden_grad_of(node("far", near_grad), chunks[1:], weight_hbm, spot)
    a2 = node("a2.g", a2_raw)
    held = jnp.concatenate([held[:2], a2], axis=1)
    a4_raw = xor_permute(node("a4.s", held[1]), "seq", 4)
    kv.take()
    states, hidden, attn_grad, qg_own, qg_send = kernel_call(
        "forward",
        forward_body,
        (
            shaped((2,) + square, bf16),
            shaped((rows, width), bf16),
            shaped((pair, length, width), bf16),
            shaped(square, f32),
            shaped((2,) + square, bf16),
        ),
        (queries, keys, values, node("forward", hidden_grad), kv_own, kv.below, kv.above),
    )
    qg = Scan("qg", qg_own, qg_send)
    qg.put(1)
    h2_raw = xor_permute(node("h2.s", hidden), "seq", 2)
    h4_raw = xor_permute(node("h4.s", hidden), "seq", 4)
    away = project(node("away", hidden), by_columns, range(1, n_head, 2), bf16)
    rs1_raw = xor_permute(node("rs1.s", away), "head", 1)
    home = project(node("home", hidden), by_columns, range(0, n_head, 2), f32)
    qg.take()
    qg.put(2)
    h2 = node("h2.g", h2_raw)
    first_rows = stacked([hidden, h2])
    hy_raw = xor_permute(node("hy.s", first_rows), "seq", 1)
    rs1 = node("rs1.g", rs1_raw)
    total = (home + rs1.astype(f32)).reshape(2, rows, own_cols)
    rs2_raw = xor_permute(node("rs2.s", total[1].astype(bf16)), "head", 2)

    query_grad, key_part, value_part = kernel_call(
        "inside",
        inside_body,
        (
            shaped((pair, length, width), bf16),
            shaped((pair, length, width), f32),
            shaped((pair, length, width), f32),
        ),
        (queries, keys, values, node("inside", attn_grad), states),
    )
    ups = jnp.concatenate([held[0], node("a4.g", a4_raw)])
    h4 = node("h4.g", h4_raw)
    g2_raw = xor_permute(node("g2.s", ups), "head", 2)
    h6_raw = xor_permute(node("h6.s", h4), "seq", 2)
    h6 = node("h6.g", h6_raw)
    second_rows = stacked([h4, h6])
    hz_raw = xor_permute(node("hz.s", second_rows), "seq", 1)
    g1_raw = xor_permute(node("g1.s", ups), "head", 1)
    qg.take()
    qg.put(4)
    g2 = node("g2.g", g2_raw)
    g3_raw = xor_permute(node("g3.s", g2), "head", 1)
    hy = node("hy.g", hy_raw)
    g1 = node("g1.g", g1_raw)
    rs2 = node("rs2.g", rs2_raw)
    qg.take()
    hz = node("hz.g", hz_raw)
    g3 = node("g3.g", g3_raw)
    ups = jnp.stack([ups, g1, g2, g3])
    key_grad, value_grad, output, weight_grad = last_call(
        [[0, 2], [1, 3], [4, 6], [5, 7]],
        (
            shaped((pair, length, width), bf16),
            shaped((pair, length, width), bf16),
            shaped((rows, own_cols), bf16),
            shaped((width, own_cols // 2), f32),
        ),
        spot,
        [keys, values, node("final", key_part), value_part, qg_own, qg.below, qg.above, total[0], rs2]
        + [first_rows, hy, second_rows, hz, ups],
    )
    return (
        output.reshape(pair, length, -1),
        query_grad,
        key_grad,
        value_grad,
        weight_grad,
    )


def carried_in(shard, axis, join, neutral, backward):
    count = lax.axis_size(axis)
    place = lax.axis_index(axis)
    ahead = count - 1 - place if backward else place
    gathered = lax.all_gather(shard.astype(jnp.bfloat16), axis)
    state = jnp.zeros_like(shard) + jnp.asarray(neutral, shard.dtype)

    def one(lap, state):
        source = count - 1 - lap if backward else lap
        return join(state, lax.dynamic_index_in_dim(gathered, source, 0, False).astype(shard.dtype))

    return lax.fori_loop(0, ahead, one, state)


def add_terms(earlier, later):
    return jax.tree.map(lambda left, right: left + right, earlier, later)


def on_any_mesh(queries, keys, values, out_weight, upstream):
    pair, length, width = queries.shape
    heads_here = width // HEAD_DIM
    shape_four = (pair, length, heads_here, HEAD_DIM)
    query4 = queries.reshape(shape_four)
    key4 = keys.reshape(shape_four)
    value4 = values.reshape(shape_four)
    kv_terms = jnp.einsum("pchd,pche->phde", key4, value4, preferred_element_type=jnp.float32)
    first_kv = kv_terms[0]
    second_kv = kv_terms[1]
    zero_state = jnp.zeros_like(first_kv)
    before = carried_in(first_kv, "seq", add_terms, zero_state, False)
    after = carried_in(second_kv, "seq", add_terms, zero_state, True)
    total_first = lax.psum(first_kv, "seq")
    state_second = total_first + after
    states = jnp.stack([before, state_second]).astype(jnp.bfloat16)
    mask = lower(length)
    scores = jnp.einsum("pthd,pshd->phts", query4, key4, preferred_element_type=jnp.float32)
    weights = jnp.where(mask, scores, 0.0).astype(jnp.bfloat16)
    attended = jnp.einsum("phts,pshe->pthe", weights, value4, preferred_element_type=jnp.float32)
    attended = attended + jnp.einsum(
        "pthd,phde->pthe", query4, states, preferred_element_type=jnp.float32
    )
    scale = jnp.sqrt(jnp.mean(attended * attended, axis=-1, keepdims=True) + EPS)
    normed = attended / scale
    hidden = normed.astype(jnp.bfloat16).reshape(pair * length, width)
    partial_out = jnp.dot(hidden, out_weight, preferred_element_type=jnp.float32)
    output = lax.psum_scatter(
        partial_out.astype(jnp.bfloat16), "head", scatter_dimension=1, tiled=True
    ).astype(jnp.float32)
    output = output.astype(jnp.bfloat16).reshape(pair, length, -1)
    flat_up = upstream.reshape(pair * length, upstream.shape[2])
    full_up = lax.all_gather(flat_up, "head", axis=1, tiled=True)
    hidden_grad = lax.dot_general(
        full_up, out_weight, (((1,), (1,)), ((), ())), preferred_element_type=jnp.float32
    )
    weight_share = lax.psum_scatter(
        lax.dot_general(
            full_up, hidden, (((0,), (0,)), ((), ())), preferred_element_type=jnp.float32
        ),
        "seq",
        scatter_dimension=0,
        tiled=True,
    )
    weight_grad = weight_share.T
    grad_four = hidden_grad.reshape(shape_four)
    inner = jnp.mean(grad_four * normed, axis=-1, keepdims=True)
    attn_grad = ((grad_four - normed * inner) / scale).astype(jnp.bfloat16)
    qg_terms = jnp.einsum("pthd,pthe->phde", query4, attn_grad, preferred_element_type=jnp.float32)
    first_qg = qg_terms[0]
    second_qg = qg_terms[1]
    higher_first = carried_in(first_qg, "seq", add_terms, zero_state, True)
    grad_second = carried_in(second_qg, "seq", add_terms, zero_state, False)
    total_second_qg = lax.psum(second_qg, "seq")
    grad_first = total_second_qg + higher_first
    later = jnp.stack([grad_first, grad_second]).astype(jnp.bfloat16)
    diffs = jnp.einsum("pthe,pshe->phts", attn_grad, value4, preferred_element_type=jnp.float32)
    diffs = jnp.where(mask, diffs, 0.0).astype(jnp.bfloat16)
    query_grad = jnp.einsum("phts,pshd->pthd", diffs, key4, preferred_element_type=jnp.float32)
    query_grad = query_grad + jnp.einsum(
        "pthe,phde->pthd", attn_grad, states, preferred_element_type=jnp.float32
    )
    key_grad = jnp.einsum("phts,pthd->pshd", diffs, query4, preferred_element_type=jnp.float32)
    key_grad = key_grad + jnp.einsum(
        "pshe,phde->pshd", value4, later, preferred_element_type=jnp.float32
    )
    value_grad = jnp.einsum(
        "phts,pthe->pshe", weights, attn_grad, preferred_element_type=jnp.float32
    )
    value_grad = value_grad + jnp.einsum(
        "pshd,phde->pshe", key4, later, preferred_element_type=jnp.float32
    )
    out_shape = (pair, length, width)
    return (
        output,
        query_grad.astype(jnp.bfloat16).reshape(out_shape),
        key_grad.astype(jnp.bfloat16).reshape(out_shape),
        value_grad.astype(jnp.bfloat16).reshape(out_shape),
        weight_grad,
    )


def on_device(*args):
    plan = on_eight_by_four if (lax.axis_size("seq"), lax.axis_size("head")) == (8, 4) else on_any_mesh
    return plan(*args)


def solution(mesh):
    rows = P(None, "seq", "head")
    return jax.shard_map(
        on_device,
        mesh=mesh,
        in_specs=(rows, rows, rows, P("head", None), rows),
        out_specs=(rows, rows, rows, rows, P("head", "seq")),
        check_vma=False,
    )
```
